256 devices in a mesh: dom: 8 (over z), shard: 32 (over x, y, core).
Axes of the slice: x: 4, y: 4, z: 8, core: 2. Of those that a mesh axis runs over, the one named last changes fastest.
Arguments:
- embedding: float32 [32768, 400], P(('dom', 'shard')), may hold values from -0.9 to 0.9
- accumulator: float32 [32768], P(('dom', 'shard')), may hold values from 0.1 to 1
- relation: float32 [16, 400], replicated, may hold values from 0.1 to 1.9
- plan: int32 [8], replicated, may hold values from 0 to 7, as said below
- lhs_index: int32 [393216], P(('dom', 'shard')), may hold values from 0 to 127
- rhs_index: int32 [393216], P(('dom', 'shard')), may hold values from 0 to 127
- rel_index: int32 [393216], P(('dom', 'shard')), may hold values from 0 to 15
- slot_count: int32 [256, 32], P(('dom', 'shard')), may hold values from 1 to 48, as said below
- neg_span: int32 [768], P(('dom', 'shard')), may hold values from 0 to 2
Outputs:
- entity_grad: float32 [32768, 400], P(('dom', 'shard'))
- adagrad_state: float32 [32768], P(('dom', 'shard'))
- relation_grad: float32 [16, 400], replicated
The draws below stay inside these ranges and needn't reach their ends.
Inputs may be any that keep to these rules, and one draw needn't show every extreme that they name: plan[d] = d XOR m for one m of 1 to 8 - 1, the same for all d. `slot_count`: every row of groups has some full slot.
All inputs are finite; a program needn't handle non-finite values.
Results may differ from the reference program's by a relative error of at most 0.00079.
Values sent between devices are 32-bit elements; how exact they have to be, the bound alone decides.
No kernel may reach another device: no remote copies, remote signals or barrier semaphores. Data moves between devices by JAX's collectives and lax.ppermute only.
A program may use at most 64 MiB of HBM per device.

```python
import math
import jax
import jax.numpy as jnp
from jax import lax

W = 400
NREL = 16
R = 128
E = 1536
CH = 512
SLOT = 48
SPANS = 3
ROWS = 32768
EDGES = 393216
N_DOM = 8
N_SHARD = 32


def draw_embedding(key, part):
    key = jax.random.fold_in(key, 11)
    base_key = jax.random.fold_in(key, 0)
    values = jnp.clip(0.15 * jax.random.normal(base_key, (ROWS, W), jnp.float32), -0.9, 0.9)
    return values.astype(jnp.float32)


def draw_plan(key, part):
    key = jax.random.fold_in(key, 23)
    flip_mask = jax.random.randint(key, (), 1, N_DOM, dtype=jnp.int32)
    return jnp.bitwise_xor(jnp.arange(N_DOM, dtype=jnp.int32), flip_mask).astype(jnp.int32)


def draw_slot_count(key, part):
    key = jax.random.fold_in(key, 37)
    count_key, full_key, shared_key, single_key = jax.random.split(key, 4)
    lowest = max(SLOT // 4, 1)
    counts = jax.random.randint(count_key, (N_DOM * N_SHARD, N_SHARD), lowest, SLOT + 1, dtype=jnp.int32)
    full_slot = jax.random.randint(full_key, (N_DOM * N_SHARD, 1), 0, N_SHARD, dtype=jnp.int32)
    shared_slot = jax.random.randint(shared_key, (), 0, N_SHARD, dtype=jnp.int32)
    single_row = jax.random.randint(single_key, (), 0, N_DOM * N_SHARD, dtype=jnp.int32)
    columns = jnp.arange(N_SHARD, dtype=jnp.int32)[None, :]
    rows_seen = jnp.arange(N_DOM * N_SHARD, dtype=jnp.int32)[:, None]
    counts = jnp.where(columns == full_slot, SLOT, counts)
    counts = jnp.where(columns == shared_slot, SLOT, counts)
    single_col = (shared_slot + 1) % N_SHARD
    counts = jnp.where((rows_seen == single_row) & (columns == single_col), 1, counts)
    return counts.astype(jnp.int32)


def with_ends(drawn, rng, smallest, top_value):
    spot = [jax.random.randint(jax.random.fold_in(rng, axis), (), 0, length) for axis, length in enumerate(drawn.shape)]
    widest = drawn.shape.index(max(drawn.shape))
    beside = spot[:widest] + [(spot[widest] + 1) % drawn.shape[widest]] + spot[widest + 1:]
    return drawn.at[tuple(spot)].set(smallest).at[tuple(beside)].set(top_value)


def shard_levels(own_key, shape, cuts, smallest, high):
    loudness = 1.0
    for axis_at, shards_of in cuts:
        heights = jax.random.uniform(jax.random.fold_in(jax.random.fold_in(own_key, 6), axis_at), (shards_of,), jnp.float32, smallest / len(cuts), high / len(cuts))
        loudness = loudness * jnp.repeat(jnp.exp(heights), shape[axis_at] // shards_of).reshape((-1,) + (1,) * (len(shape) - 1 - axis_at))
    return loudness


def setup_inputs(seed: int = 0) -> dict:
    splits = jax.random.split(jax.random.key(seed), 10)
    embedding = draw_embedding(jax.random.fold_in(splits[9], 71), 0)
    accumulator = jnp.clip(jnp.exp(math.log(1.0) - 2.3025851 * jax.random.uniform(splits[1], (ROWS,), jnp.float32) ** shard_levels(splits[1], (ROWS,), ((0, 256),), -0.2, 0.2)), 0.1, 1.0)
    relation = jnp.clip(1.0 + 0.18 * jax.random.normal(splits[2], (NREL, W), jnp.float32), 0.1, 1.9)
    plan = draw_plan(jax.random.fold_in(splits[9], 71), 0)
    lhs_index = with_ends(jax.random.randint(splits[4], (EDGES,), 0, R), jax.random.fold_in(splits[4], 1), 0, R - 1).astype(jnp.int32)
    rhs_index = with_ends(jax.random.randint(splits[5], (EDGES,), 0, R), jax.random.fold_in(splits[5], 1), 0, R - 1).astype(jnp.int32)
    rel_index = with_ends(jax.random.randint(splits[6], (EDGES,), 0, NREL), jax.random.fold_in(splits[6], 1), 0, NREL - 1).astype(jnp.int32)
    slot_count = draw_slot_count(jax.random.fold_in(splits[9], 71), 0)
    neg_span = with_ends(jax.random.randint(splits[8], (N_DOM * N_SHARD * SPANS,), 0, SPANS), jax.random.fold_in(splits[8], 1), 0, SPANS - 1).astype(jnp.int32)
    return {"embedding": embedding, "accumulator": accumulator, "relation": relation, "plan": plan, "lhs_index": lhs_index, "rhs_index": rhs_index, "rel_index": rel_index, "slot_count": slot_count, "neg_span": neg_span}


def soft_weights(positive, scores, live_cols):
    masked = jnp.where(live_cols, scores, -jnp.inf)
    row_max = jnp.maximum(positive, jnp.max(masked, axis=1))
    own_term = jnp.exp(positive - row_max)
    others = jnp.exp(masked - row_max[:, None])
    summed = own_term + jnp.sum(others, axis=1)
    return others / summed[:, None], own_term / summed


def add_rows(values, first_row, update):
    current = lax.dynamic_slice_in_dim(values, first_row, update.shape[0], 0)
    return lax.dynamic_update_slice_in_dim(values, current + update, first_row, 0)


def edge_grads(lhs_rows, rel_rows, rhs_rows, valid_rows, negatives, block_size):
    block_count = lhs_rows.shape[0] // block_size
    inner = (((1,), (1,)), ((), ()))
    outer = (((0,), (0,)), ((), ()))

    def one_block(block_index, grad_parts):
        grad_lhs, grad_rhs, grad_rel = grad_parts
        first_row = (block_index * block_size).astype(jnp.int32)
        neg_first = (negatives[block_index] * block_size).astype(jnp.int32)
        lhs_here = lax.dynamic_slice_in_dim(lhs_rows, first_row, block_size, 0)
        rhs_here = lax.dynamic_slice_in_dim(rhs_rows, first_row, block_size, 0)
        rel_here = lax.dynamic_slice_in_dim(rel_rows, first_row, block_size, 0)
        live_here = lax.dynamic_slice_in_dim(valid_rows, first_row, block_size, 0)
        lhs_neg = lax.dynamic_slice_in_dim(lhs_rows, neg_first, block_size, 0).astype(jnp.bfloat16)
        rhs_neg = lax.dynamic_slice_in_dim(rhs_rows, neg_first, block_size, 0).astype(jnp.bfloat16)
        live_neg = lax.dynamic_slice_in_dim(valid_rows, neg_first, block_size, 0)
        left = lhs_here * rel_here
        right = rhs_here * rel_here
        positive = jnp.sum(left * rhs_here, axis=1)
        left_b = left.astype(jnp.bfloat16)
        right_b = right.astype(jnp.bfloat16)
        tail_scores = lax.dot_general(left_b, rhs_neg, inner, preferred_element_type=jnp.float32)
        head_scores = lax.dot_general(right_b, lhs_neg, inner, preferred_element_type=jnp.float32)
        live_cols = live_neg[None, :] > 0.5
        tail_prob, tail_pos = soft_weights(positive, tail_scores, live_cols)
        head_prob, head_pos = soft_weights(positive, head_scores, live_cols)
        weight_pos = live_here * (tail_pos + head_pos - 2.0)
        tail_w = (live_here[:, None] * tail_prob).astype(jnp.bfloat16)
        head_w = (live_here[:, None] * head_prob).astype(jnp.bfloat16)
        grad_left = weight_pos[:, None] * rhs_here + jnp.dot(tail_w, rhs_neg, preferred_element_type=jnp.float32)
        grad_right = jnp.dot(head_w, lhs_neg, preferred_element_type=jnp.float32)
        grad_lhs = add_rows(grad_lhs, first_row, grad_left * rel_here)
        grad_rhs = add_rows(grad_rhs, first_row, weight_pos[:, None] * left + grad_right * rel_here)
        grad_rel = add_rows(grad_rel, first_row, grad_left * lhs_here + grad_right * rhs_here)
        grad_rhs = add_rows(grad_rhs, neg_first, lax.dot_general(tail_w, left_b, outer, preferred_element_type=jnp.float32))
        grad_lhs = add_rows(grad_lhs, neg_first, lax.dot_general(head_w, right_b, outer, preferred_element_type=jnp.float32))
        return (grad_lhs, grad_rhs, grad_rel)

    empty_grad = jnp.zeros_like(lhs_rows)
    return lax.fori_loop(0, block_count, one_block, (empty_grad, empty_grad, empty_grad))


def reference(embedding, accumulator, relation, plan, lhs_index, rhs_index, rel_index, slot_count, neg_span):
    group_count = N_DOM * N_SHARD
    lhs_groups = lhs_index.reshape(group_count, E)
    rhs_groups = rhs_index.reshape(group_count, E)
    rel_groups = rel_index.reshape(group_count, E)
    neg_groups = neg_span.reshape(group_count, SPANS)

    def one_group(running, inputs):
        table_grad, rel_grad = running
        group, lhs_local, rhs_local, rel_local, counts, negatives = inputs
        dom_index = group // N_SHARD
        partner = plan[dom_index]
        owner_shard = jnp.arange(E, dtype=jnp.int32) // SLOT
        lhs_global = (group * R + lhs_local).astype(jnp.int32)
        rhs_global = ((partner * N_SHARD + owner_shard) * R + rhs_local).astype(jnp.int32)
        valid_rows = (jnp.arange(SLOT, dtype=jnp.int32)[None, :] < counts[:, None]).reshape(E).astype(embedding.dtype)
        lhs_rows = embedding[lhs_global]
        rhs_rows = embedding[rhs_global]
        rel_rows = relation[rel_local]
        grad_lhs, grad_rhs, grad_rel = edge_grads(lhs_rows, rel_rows, rhs_rows, valid_rows, negatives, CH)
        table_grad = table_grad.at[lhs_global].add(grad_lhs).at[rhs_global].add(grad_rhs)
        rel_grad = rel_grad.at[rel_local].add(grad_rel)
        return (table_grad, rel_grad), None

    groups = jnp.arange(group_count, dtype=jnp.int32)
    start_state = (jnp.zeros_like(embedding), jnp.zeros_like(relation))
    (table_grad, rel_grad), _ = lax.scan(one_group, start_state, (groups, lhs_groups, rhs_groups, rel_groups, slot_count, neg_groups))
    adagrad_state = accumulator + jnp.mean(table_grad * table_grad, axis=1)
    return (table_grad, adagrad_state, rel_grad)
```

```python
import functools

import jax
import jax.numpy as jnp
from jax import lax
from jax.experimental import pallas as pl
from jax.experimental.pallas import tpu as pltpu
from jax.sharding import PartitionSpec as P

W = 400
R = 128
E = 1536
CH = 512
SLOT = 48
SPANS = 3
N_DOM = 8
N_SHARD = 32
TILE = 256
TILES = E // TILE
SPREAD = 6
FIRST = [TILE * j // SLOT for j in range(TILES)]
PACK = 56
F32 = jnp.float32
BF16 = jnp.bfloat16
NT = (((1,), (1,)), ((), ()))
NN = (((1,), (0,)), ((), ()))


def dot(a, b, dims=NN):
    return lax.dot_general(a, b, dims, preferred_element_type=F32)


def split(x):
    hi = x.astype(BF16)
    return hi, (x - hi.astype(F32)).astype(BF16)


def onehot(mask):
    return jnp.where(mask, 1.0, 0.0).astype(BF16)


def rows_of(z_ref, first, j):
    return jnp.concatenate([z_ref[first + 2 * j : first + 2 * j + 1, :], z_ref[first + 2 * j + 1 : first + 2 * j + 2, :]], axis=1)


def main_kernel(slot_ref, neg_ref, z_ref, rel_ref, *refs):
    pieces = refs[:10]
    p_out = refs[10:18]
    lg_ref, rg_ref = refs[18:20]
    hi_s, lo_s, lhs_s, rel_s, rhs_s, gl_s, gr_s, lhsb_s, rhsb_s, lhsr_s, rhsr_s, bias_s, p_s = refs[20:]

    for side in range(2):
        for k, (piece, places) in enumerate(zip(pieces[5 * side : 5 * side + 5], PLACES)):
            for i, place in enumerate(places):
                lanes = pl.ds(pl.multiple_of(slot_ref[16 * side + place] * R, R), R)
                hi, lo = split(piece[i])
                hi_s[:, lanes] = hi
                lo_s[:, lanes] = lo

    zt = jnp.concatenate([z_ref[W : W + PACK, :], jnp.zeros((R - PACK, R), F32)], axis=0).T
    lt_hi, lt_lo = split(z_ref[:W, :])
    sub_iota = lax.broadcasted_iota(jnp.int32, (SPREAD * R, TILE), 0).astype(F32)
    lane_iota = lax.broadcasted_iota(jnp.int32, (R, SPREAD * R), 1).astype(F32)
    rel_iota = lax.broadcasted_iota(jnp.int32, (R, TILE), 0)
    rel_iota = jnp.where(rel_iota < 48, rel_iota % 16, -1).astype(F32)

    rel = rel_ref[...]
    part = lax.broadcasted_iota(jnp.int32, (W, R), 1) // 16
    hi = rel.astype(BF16).astype(F32)
    mid = (rel - hi).astype(BF16).astype(F32)
    low = rel - hi - mid
    rel3 = jnp.where(part == 0, hi, jnp.where(part == 1, mid, jnp.where(part == 2, low, 0.0))).astype(BF16)

    for j in range(TILES):
        c, at = divmod(j * TILE, CH)
        lanes = slice(at, at + TILE)
        base = FIRST[j] * R
        oh = onehot(sub_iota == rows_of(z_ref, W + 12, j) - float(base))
        cols = slice(base, base + SPREAD * R)
        rhs = dot(hi_s[:, cols], oh) + dot(lo_s[:, cols], oh)
        rhs_s[c, :, lanes] = rhs
        rhsb_s[c, :, lanes] = rhs.astype(BF16)
        ohr = jnp.concatenate(
            [onehot(lane_iota == zt[:, 12 + 2 * j + i : 13 + 2 * j + i] - float(base)) for i in range(2)], axis=0
        )
        rhsr_s[c, lanes, :] = dot(ohr, hi_s[:, cols], NT).astype(BF16)
        oh = onehot(sub_iota[:R] == rows_of(z_ref, W, j))
        lhs = dot(lt_hi, oh) + dot(lt_lo, oh)
        lhs_s[c, :, lanes] = lhs
        lhsb_s[c, :, lanes] = lhs.astype(BF16)
        ohr = jnp.concatenate([onehot(lane_iota[:, :R] == zt[:, 2 * j + i : 1 + 2 * j + i]) for i in range(2)], axis=0)
        lhsr_s[c, lanes, :] = dot(ohr, lt_hi, NT).astype(BF16)
        oh = onehot(rel_iota == rows_of(z_ref, W + 24, j))
        rel_s[c, :, lanes] = dot(rel3, oh)
        for i in range(2):
            live = jnp.broadcast_to(zt[:, 36 + 2 * j + i : 37 + 2 * j + i], (R, R))
            bias_s[c, at + i * R : at + (i + 1) * R, :] = jnp.where(live > 0.5, 0.0, -jnp.inf)

    gl_s[...] = jnp.zeros_like(gl_s)
    gr_s[...] = jnp.zeros_like(gr_s)
    rel_grad = jnp.zeros((16, W), F32)
    rel_rows = lax.broadcasted_iota(jnp.int32, (16, CH), 0).astype(F32)
    for c in range(SPANS):
        n = neg_ref[c]
        lhs, rel, rhs = lhs_s[c], rel_s[c], rhs_s[c]
        left, right = lhs * rel, rhs * rel
        positive = jnp.sum(left * rhs, axis=0, keepdims=True)
        leftb, rightb = left.astype(BF16), right.astype(BF16)
        live = jnp.concatenate([rows_of(z_ref, W + 36, 2 * c), rows_of(z_ref, W + 36, 2 * c + 1)], axis=1)
        bias = jnp.concatenate([bias_s[n]] * 4, axis=1)

        def soft(neg_rows, edges):
            scores = dot(neg_rows, edges) + bias
            top = jnp.maximum(positive, jnp.max(scores, axis=0, keepdims=True))
            own = jnp.exp(positive - top)
            others = jnp.exp(scores - top)
            inv = 1.0 / (own + jnp.sum(others, axis=0, keepdims=True))
            return (others * (live * inv)).astype(BF16), own * inv

        tail_w, q_tail = soft(rhsr_s[n], leftb)
        head_w, q_head = soft(lhsr_s[n], rightb)
        weight = live * (q_tail + q_head - 2.0)
        grad_left = weight * rhs + dot(rhsb_s[n], tail_w)
        grad_right = dot(lhsb_s[n], head_w)
        gl_s[c] += grad_left * rel
        gr_s[c] += weight * left + grad_right * rel
        gr_s[n] += dot(leftb, tail_w, NT)
        gl_s[n] += dot(rightb, head_w, NT)
        ghi, glo = split(grad_left * lhs + grad_right * rhs)
        row = jnp.concatenate([rows_of(z_ref, W + 24, 2 * c), rows_of(z_ref, W + 24, 2 * c + 1)], axis=1)
        oh = onehot(rel_rows == row)
        rel_grad += dot(oh, ghi, NT) + dot(oh, glo, NT)
    rg_ref[...] = rel_grad

    lg = jnp.zeros((W, R), F32)
    p_s[...] = jnp.zeros_like(p_s)
    for j in range(TILES):
        c, at = divmod(j * TILE, CH)
        lanes = slice(at, at + TILE)
        base = FIRST[j] * R
        oh = onehot(sub_iota == rows_of(z_ref, W + 12, j) - float(base))
        cols = slice(base, base + SPREAD * R)
        hi, lo = split(gr_s[c, :, lanes])
        p_s[:, cols] += dot(hi, oh, NT) + dot(lo, oh, NT)
        oh = onehot(sub_iota[:R] == rows_of(z_ref, W, j))
        hi, lo = split(gl_s[c, :, lanes])
        lg += dot(hi, oh, NT) + dot(lo, oh, NT)
    lg_ref[...] = lg
    for side in range(2):
        for jq in range(4):
            out = p_out[4 * side + jq]
            for jp in range(4):
                lanes = pl.ds(pl.multiple_of(slot_ref[16 * side + 4 * jq + jp] * R, R), R)
                out[jp] = p_s[:, lanes]


PLACES = [(0, 1, 2, 3), (4, 5, 6, 7), (12, 13, 14, 15), (8, 9), (10, 11)]


def main_call(slots, neg, z, rel, pieces):
    smem = pl.BlockSpec(memory_space=pltpu.SMEM)
    vmem = pl.BlockSpec(memory_space=pltpu.VMEM)
    table = jax.ShapeDtypeStruct((4, W, R), F32)
    big = pltpu.VMEM((SPANS, W, CH), F32)
    half = pltpu.VMEM((SPANS, W, CH), BF16)
    rows = pltpu.VMEM((SPANS, CH, W), BF16)
    return pl.pallas_call(
        main_kernel,
        out_shape=[table] * 8 + [jax.ShapeDtypeStruct((W, R), F32), jax.ShapeDtypeStruct((16, W), F32)],
        in_specs=[smem, smem] + [vmem] * 12,
        out_specs=[vmem] * 10,
        scratch_shapes=[
            pltpu.VMEM((W, N_SHARD * R), BF16),
            pltpu.VMEM((W, N_SHARD * R), BF16),
            big, big, big, big, big, half, half, rows, rows,
            pltpu.VMEM((SPANS, CH, R), F32),
            pltpu.VMEM((W, N_SHARD * R), F32),
        ],
        compiler_params=pltpu.CompilerParams(vmem_limit_bytes=60 * 1024 * 1024),
        cost_estimate=pl.CostEstimate(flops=12_000_000_000, bytes_accessed=14_000_000, transcendentals=1_600_000),
        name="edges",
    )(slots, neg, z, rel, *pieces)


def last_kernel(a_ref, b_ref, acc_ref, ent_ref, state_ref):
    g = a_ref[...] + b_ref[...]
    state_ref[...] = acc_ref[...] + jnp.sum(g * g, axis=0, keepdims=True) * (1.0 / W)
    ent_ref[...] = jnp.concatenate([g, jnp.zeros((512 - W, R), F32)], axis=0).T[:, :W]


def last_call(a, b, acc):
    return pl.pallas_call(
        last_kernel,
        out_shape=[jax.ShapeDtypeStruct((R, W), F32), jax.ShapeDtypeStruct((1, R), F32)],
        name="last",
    )(a, b, acc)


def step_pairs(first, second):
    pairs = []
    for s in range(N_SHARD):
        x, y, c = s // 8, (s // 2) % 4, s % 2
        dx, dy = (first, second) if c == 0 else (second, first)
        pairs.append((s, (((x + dx) % 4) * 4 + (y + dy) % 4) * 2 + c))
    return pairs


def move(value, first=0, second=0):
    return lax.ppermute(value, "shard", step_pairs(first, second))


def swap_core(value):
    return lax.ppermute(value, "shard", [(s, s ^ 1) for s in range(N_SHARD)])


def swap_dom(value, mask):
    return lax.ppermute(value, "dom", [(d, d ^ mask) for d in range(N_DOM)])


def gather_tables(t):
    x1 = jnp.stack([t, move(t, first=-1), move(t, first=2), move(t, first=1)])
    o1, o3 = move(x1, second=-1), move(x1, second=1)
    f2, g2 = move(o3[:2], second=1), move(o1[2:], second=-1)
    own = [x1, o1, o3, f2, g2]
    return own + [swap_core(v) for v in own]


def reduce_tables(p):
    own, sib = p[:4], p[4:]
    own = [own[k] + swap_core(sib[k]) for k in range(4)]
    up, down = move(own[2][:2], second=1), move(own[2][2:], second=-1)
    one = jnp.concatenate([own[1][:2] + up, own[1][2:]])
    three = jnp.concatenate([own[3][:2], own[3][2:] + down])
    y = own[0] + move(one, second=1) + move(three, second=-1)
    return y[0] + move(y[1], first=1) + move(y[3], first=-1) + move(y[2], first=2)


def sum_all(value):
    for mask in (1, 2, 4, 8, 16):
        value = value + lax.ppermute(value, "shard", [(s, s ^ mask) for s in range(N_SHARD)])
    for mask in (1, 2, 4):
        value = value + swap_dom(value, mask)
    return value


def local(embedding, accumulator, relation, plan, lhs_index, rhs_index, rel_index, slot_count, neg_span):
    shard = lax.axis_index("shard")
    x, y, c = shard // 8, (shard // 2) % 4, shard % 2
    j = jnp.arange(16, dtype=jnp.int32)
    jq, jp = j // 4, j % 4

    def owners(core):
        dx, dy = jnp.where(core == 0, jp, jq), jnp.where(core == 0, jq, jp)
        return (((x + dx) % 4) * 4 + (y + dy) % 4) * 2 + core

    slots = jnp.concatenate([owners(c), owners(1 - c)]).astype(jnp.int32)

    table = embedding.T
    owner = jnp.arange(E, dtype=jnp.int32) // SLOT
    live = (jnp.arange(SLOT, dtype=jnp.int32)[None, :] < slot_count[0][:, None]).reshape(12, R)
    pack = [lhs_index.reshape(12, R), (owner * R + rhs_index).reshape(12, R), rel_index.reshape(12, R), live]
    pack = [v.astype(F32) for v in pack]
    pack.append(jnp.zeros((PACK - 48, R), F32).at[0, :SPANS].set(neg_span.astype(F32)))
    payload = jnp.concatenate([table] + pack)

    rel = jnp.concatenate([relation] * 8).T

    def run(mask):
        z = swap_dom(payload, mask)
        neg = z[W + 48, :SPANS].astype(jnp.int32)
        pieces = gather_tables(table)
        *p, lhs_grad, rel_grad = main_call(slots, neg, z, rel, pieces)
        lhs_grad = swap_dom(lhs_grad, mask)
        total = reduce_tables(p)
        entity_grad, state = last_call(total, lhs_grad, accumulator.reshape(1, R))
        return entity_grad, state.reshape(R), sum_all(rel_grad)

    return lax.switch(plan[0] - 1, [functools.partial(run, m) for m in range(1, N_DOM)])


def solution(mesh):
    both = P(("dom", "shard"))
    rows = P(("dom", "shard"), None)
    in_specs = (rows, both, P(), P(), both, both, both, rows, both)
    return jax.shard_map(local, mesh=mesh, in_specs=in_specs, out_specs=(rows, both, P()), check_vma=False)
```

```python
import jax
import jax.numpy as jnp
from jax import lax
from jax.experimental import pallas as pl
from jax.experimental.pallas import tpu as pltpu
from jax.sharding import PartitionSpec as P

W = 400
R = 128
E = 1536
CH = 512
SLOT = 48
SPANS = 3
N_DOM = 8
N_SHARD = 32
TILE = 256
TILES = E // TILE
SPREAD = 6
FIRST = [TILE * j // SLOT for j in range(TILES)]
PACK = 56
F32 = jnp.float32
BF16 = jnp.bfloat16
NT = (((1,), (1,)), ((), ()))
NN = (((1,), (0,)), ((), ()))


def dot(a, b, dims=NN):
    return lax.dot_general(a, b, dims, preferred_element_type=F32)


def split(x):
    hi = x.astype(BF16)
    return hi, (x - hi.astype(F32)).astype(BF16)


def onehot(mask):
    return jnp.where(mask, 1.0, 0.0).astype(BF16)


def rows_of(z_ref, first, j):
    return jnp.concatenate([z_ref[first + 2 * j : first + 2 * j + 1, :], z_ref[first + 2 * j + 1 : first + 2 * j + 2, :]], axis=1)


def main_kernel(slot_ref, neg_ref, z_ref, rel_ref, *refs):
    pieces = refs[:10]
    p_out = refs[10:18]
    lg_ref, rg_ref = refs[18:20]
    hi_s, lo_s, lhs_s, rel_s, rhs_s, gl_s, gr_s, lhsb_s, rhsb_s, lhsr_s, rhsr_s, bias_s, p_s = refs[20:]

    for side in range(2):
        for k, (piece, places) in enumerate(zip(pieces[5 * side : 5 * side + 5], PLACES)):
            for i, place in enumerate(places):
                lanes = pl.ds(pl.multiple_of(slot_ref[16 * side + place] * R, R), R)
                hi, lo = split(piece[i])
                hi_s[:, lanes] = hi
                lo_s[:, lanes] = lo

    zt = jnp.concatenate([z_ref[W : W + PACK, :], jnp.zeros((R - PACK, R), F32)], axis=0).T
    lt_hi, lt_lo = split(z_ref[:W, :])
    sub_iota = lax.broadcasted_iota(jnp.int32, (SPREAD * R, TILE), 0).astype(F32)
    lane_iota = lax.broadcasted_iota(jnp.int32, (R, SPREAD * R), 1).astype(F32)
    rel_iota = lax.broadcasted_iota(jnp.int32, (R, TILE), 0)
    rel_iota = jnp.where(rel_iota < 48, rel_iota % 16, -1).astype(F32)

    rel = rel_ref[...]
    part = lax.broadcasted_iota(jnp.int32, (W, R), 1) // 16
    hi = rel.astype(BF16).astype(F32)
    mid = (rel - hi).astype(BF16).astype(F32)
    low = rel - hi - mid
    rel3 = jnp.where(part == 0, hi, jnp.where(part == 1, mid, jnp.where(part == 2, low, 0.0))).astype(BF16)

    for j in range(TILES):
        c, at = divmod(j * TILE, CH)
        lanes = slice(at, at + TILE)
        base = FIRST[j] * R
        oh = onehot(sub_iota == rows_of(z_ref, W + 12, j) - float(base))
        cols = slice(base, base + SPREAD * R)
        rhs = dot(hi_s[:, cols], oh) + dot(lo_s[:, cols], oh)
        rhs_s[c, :, lanes] = rhs
        rhsb_s[c, :, lanes] = rhs.astype(BF16)
        ohr = jnp.concatenate(
            [onehot(lane_iota == zt[:, 12 + 2 * j + i : 13 + 2 * j + i] - float(base)) for i in range(2)], axis=0
        )
        rhsr_s[c, lanes, :] = dot(ohr, hi_s[:, cols], NT).astype(BF16)
        oh = onehot(sub_iota[:R] == rows_of(z_ref, W, j))
        lhs = dot(lt_hi, oh) + dot(lt_lo, oh)
        lhs_s[c, :, lanes] = lhs
        lhsb_s[c, :, lanes] = lhs.astype(BF16)
        ohr = jnp.concatenate([onehot(lane_iota[:, :R] == zt[:, 2 * j + i : 1 + 2 * j + i]) for i in range(2)], axis=0)
        lhsr_s[c, lanes, :] = dot(ohr, lt_hi, NT).astype(BF16)
        oh = onehot(rel_iota == rows_of(z_ref, W + 24, j))
        rel_s[c, :, lanes] = dot(rel3, oh)
        for i in range(2):
            live = jnp.broadcast_to(zt[:, 36 + 2 * j + i : 37 + 2 * j + i], (R, R))
            bias_s[c, at + i * R : at + (i + 1) * R, :] = jnp.where(live > 0.5, 0.0, -jnp.inf)

    gl_s[...] = jnp.zeros_like(gl_s)
    gr_s[...] = jnp.zeros_like(gr_s)
    rel_grad = jnp.zeros((16, W), F32)
    rel_rows = lax.broadcasted_iota(jnp.int32, (16, CH), 0).astype(F32)
    for c in range(SPANS):
        n = neg_ref[c]
        lhs, rel, rhs = lhs_s[c], rel_s[c], rhs_s[c]
        left, right = lhs * rel, rhs * rel
        positive = jnp.sum(left * rhs, axis=0, keepdims=True)
        leftb, rightb = left.astype(BF16), right.astype(BF16)
        live = jnp.concatenate([rows_of(z_ref, W + 36, 2 * c), rows_of(z_ref, W + 36, 2 * c + 1)], axis=1)
        bias = jnp.concatenate([bias_s[n]] * 4, axis=1)

        def soft(neg_rows, edges):
            scores = dot(neg_rows, edges) + bias
            top = jnp.maximum(positive, jnp.max(scores, axis=0, keepdims=True))
            own = jnp.exp(positive - top)
            others = jnp.exp(scores - top)
            inv = 1.0 / (own + jnp.sum(others, axis=0, keepdims=True))
            return (others * (live * inv)).astype(BF16), own * inv

        tail_w, q_tail = soft(rhsr_s[n], leftb)
        head_w, q_head = soft(lhsr_s[n], rightb)
        weight = live * (q_tail + q_head - 2.0)
        grad_left = weight * rhs + dot(rhsb_s[n], tail_w)
        grad_right = dot(lhsb_s[n], head_w)
        gl_s[c] += grad_left * rel
        gr_s[c] += weight * left + grad_right * rel
        gr_s[n] += dot(leftb, tail_w, NT)
        gl_s[n] += dot(rightb, head_w, NT)
        ghi, glo = split(grad_left * lhs + grad_right * rhs)
        row = jnp.concatenate([rows_of(z_ref, W + 24, 2 * c), rows_of(z_ref, W + 24, 2 * c + 1)], axis=1)
        oh = onehot(rel_rows == row)
        rel_grad += dot(oh, ghi, NT) + dot(oh, glo, NT)
    tail = jnp.concatenate([rel_grad[:, 384:], jnp.zeros((16, R - 16), F32)], axis=1)
    rg_ref[...] = jnp.concatenate([rel_grad[:, :R], rel_grad[:, R : 2 * R], rel_grad[:, 2 * R : 3 * R], tail], axis=0)

    lg = jnp.zeros((W, R), F32)
    p_s[...] = jnp.zeros_like(p_s)
    for j in range(TILES):
        c, at = divmod(j * TILE, CH)
        lanes = slice(at, at + TILE)
        base = FIRST[j] * R
        oh = onehot(sub_iota == rows_of(z_ref, W + 12, j) - float(base))
        cols = slice(base, base + SPREAD * R)
        hi, lo = split(gr_s[c, :, lanes])
        p_s[:, cols] += dot(hi, oh, NT) + dot(lo, oh, NT)
        oh = onehot(sub_iota[:R] == rows_of(z_ref, W, j))
        hi, lo = split(gl_s[c, :, lanes])
        lg += dot(hi, oh, NT) + dot(lo, oh, NT)
    lg_ref[...] = lg
    for side in range(2):
        for jq in range(4):
            out = p_out[4 * side + jq]
            for jp in range(4):
                lanes = pl.ds(pl.multiple_of(slot_ref[16 * side + 4 * jq + jp] * R, R), R)
                out[jp] = p_s[:, lanes]


PLACES = [(0, 1, 2, 3), (4, 5, 6, 7), (12, 13, 14, 15), (8, 9), (10, 11)]


def main_call(slots, neg, z, rel, pieces):
    smem = pl.BlockSpec(memory_space=pltpu.SMEM)
    vmem = pl.BlockSpec(memory_space=pltpu.VMEM)
    table = jax.ShapeDtypeStruct((4, W, R), F32)
    big = pltpu.VMEM((SPANS, W, CH), F32)
    half = pltpu.VMEM((SPANS, W, CH), BF16)
    rows = pltpu.VMEM((SPANS, CH, W), BF16)
    return pl.pallas_call(
        main_kernel,
        out_shape=[table] * 8 + [jax.ShapeDtypeStruct((W, R), F32), jax.ShapeDtypeStruct((64, R), F32)],
        in_specs=[smem, smem] + [vmem] * 12,
        out_specs=[vmem] * 10,
        scratch_shapes=[
            pltpu.VMEM((W, N_SHARD * R), BF16),
            pltpu.VMEM((W, N_SHARD * R), BF16),
            big, big, big, big, big, half, half, rows, rows,
            pltpu.VMEM((SPANS, CH, R), F32),
            pltpu.VMEM((W, N_SHARD * R), F32),
        ],
        compiler_params=pltpu.CompilerParams(vmem_limit_bytes=60 * 1024 * 1024),
        cost_estimate=pl.CostEstimate(flops=12_000_000_000, bytes_accessed=14_000_000, transcendentals=1_600_000),
        name="edges",
    )(slots, neg, z, rel, *pieces)


def last_kernel(core_ref, a_ref, b_ref, acc_ref, mine_ref, other_ref, ent_ref, state_ref, rel_ref):
    g = a_ref[...] + b_ref[...]
    state_ref[...] = acc_ref[...] + jnp.sum(g * g, axis=0, keepdims=True) * (1.0 / W)
    ent_ref[...] = jnp.concatenate([g, jnp.zeros((512 - W, R), F32)], axis=0).T[:, :W]
    mine, other = mine_ref[...], other_ref[...]
    low = jnp.where(core_ref[0] == 0, mine, other)
    high = jnp.where(core_ref[0] == 0, other, mine)
    rel_ref[:, :R] = low[:16]
    rel_ref[:, R : 2 * R] = low[16:]
    rel_ref[:, 2 * R : 3 * R] = high[:16]
    rel_ref[:, 3 * R :] = high[16:, : W - 3 * R]


def last_call(core, a, b, acc, mine, other):
    smem = pl.BlockSpec(memory_space=pltpu.SMEM)
    vmem = pl.BlockSpec(memory_space=pltpu.VMEM)
    return pl.pallas_call(
        last_kernel,
        out_shape=[
            jax.ShapeDtypeStruct((R, W), F32),
            jax.ShapeDtypeStruct((1, R), F32),
            jax.ShapeDtypeStruct((16, W), F32),
        ],
        in_specs=[smem] + [vmem] * 5,
        out_specs=[vmem] * 3,
        name="last",
    )(core, a, b, acc, mine, other)


def step_pairs(first, second):
    pairs = []
    for s in range(N_SHARD):
        x, y, c = s // 8, (s // 2) % 4, s % 2
        dx, dy = (first, second) if c == 0 else (second, first)
        pairs.append((s, (((x + dx) % 4) * 4 + (y + dy) % 4) * 2 + c))
    return pairs


def move(value, first=0, second=0):
    return lax.ppermute(value, "shard", step_pairs(first, second))


def swap_core(value):
    return lax.ppermute(value, "shard", [(s, s ^ 1) for s in range(N_SHARD)])


def swap_dom(value, mask):
    return lax.ppermute(value, "dom", [(d, d ^ mask) for d in range(N_DOM)])


def pair_move(value, mask):
    for bit in (4, 2, 1):
        value = jnp.where((mask & bit) != 0, swap_dom(value, bit), value)
    return value


def gather_tables(t):
    x1 = jnp.stack([t, move(t, first=-1), move(t, first=2), move(t, first=1)])
    o1, o3 = move(x1, second=-1), move(x1, second=1)
    f2, g2 = move(o3[:2], second=1), move(o1[2:], second=-1)
    own = [x1, o1, o3, f2, g2]
    return own + [swap_core(v) for v in own]


def with_rel(tables, rel):
    return jnp.concatenate([tables.reshape(-1, R), rel])


def reduce_tables(p, rel, core):
    for mask in (1, 2, 4):
        rel = rel + swap_dom(rel, mask)
    low, high = rel[:32], rel[32:]
    mine = jnp.where(core == 0, low, high) + swap_core(jnp.where(core == 0, high, low))
    own, sib = p[:4], p[4:]
    own = {k: own[k] + swap_core(sib[k]) for k in (2, 1, 3, 0)}
    up, down = move(own[2][:2], second=1), move(own[2][2:], second=-1)
    one = jnp.concatenate([own[1][:2] + up, own[1][2:]])
    three = jnp.concatenate([own[3][:2], own[3][2:] + down])
    one, three = move(with_rel(one, mine), second=1), move(with_rel(three, mine), second=-1)
    mine = (mine + move(mine, second=2)) + (one[4 * W :] + three[4 * W :])
    y = own[0] + (one[: 4 * W] + three[: 4 * W]).reshape(4, W, R)
    one, three, two = (move(with_rel(y[k], mine), first=k) for k in (1, 3, 2))
    mine = (mine + two[W:]) + (one[W:] + three[W:])
    return y[0] + one[:W] + three[:W] + two[:W], mine


def local(embedding, accumulator, relation, plan, lhs_index, rhs_index, rel_index, slot_count, neg_span):
    shard = lax.axis_index("shard")
    x, y, c = shard // 8, (shard // 2) % 4, shard % 2
    j = jnp.arange(16, dtype=jnp.int32)
    jq, jp = j // 4, j % 4

    def owners(core):
        dx, dy = jnp.where(core == 0, jp, jq), jnp.where(core == 0, jq, jp)
        return (((x + dx) % 4) * 4 + (y + dy) % 4) * 2 + core

    slots = jnp.concatenate([owners(c), owners(1 - c)]).astype(jnp.int32)

    table = embedding.T
    owner = jnp.arange(E, dtype=jnp.int32) // SLOT
    live = (jnp.arange(SLOT, dtype=jnp.int32)[None, :] < slot_count[0][:, None]).reshape(12, R)
    pack = [lhs_index.reshape(12, R), (owner * R + rhs_index).reshape(12, R), rel_index.reshape(12, R), live]
    pack = [v.astype(F32) for v in pack]
    pack.append(jnp.zeros((PACK - 48, R), F32).at[0, :SPANS].set(neg_span.astype(F32)))
    payload = jnp.concatenate([table] + pack)

    rel = jnp.concatenate([relation] * 8).T

    mask = plan[0]
    z = pair_move(payload, mask)
    neg = z[W + 48, :SPANS].astype(jnp.int32)
    pieces = gather_tables(table)
    *p, lhs_grad, rel_grad = main_call(slots, neg, z, rel, pieces)
    lhs_grad = pair_move(lhs_grad, mask)
    total, mine = reduce_tables(p, rel_grad, c)
    core = jnp.reshape(c, (1,)).astype(jnp.int32)
    entity_grad, state, relation_grad = last_call(
        core, total, lhs_grad, accumulator.reshape(1, R), mine, swap_core(mine)
    )
    return entity_grad, state.reshape(R), relation_grad


def solution(mesh):
    both = P(("dom", "shard"))
    rows = P(("dom", "shard"), None)
    in_specs = (rows, both, P(), P(), both, both, both, rows, both)
    return jax.shard_map(local, mesh=mesh, in_specs=in_specs, out_specs=(rows, both, P()), check_vma=False)
```

```python
import functools

import jax
import jax.numpy as jnp
from jax import lax
from jax.experimental import pallas as pl
from jax.experimental.pallas import tpu as pltpu
from jax.sharding import PartitionSpec as P

W = 400
R = 128
E = 1536
CH = 512
SLOT = 48
SPANS = 3
N_DOM = 8
N_SHARD = 32
TILE = 256
TILES = E // TILE
SPREAD = 6
FIRST = [TILE * j // SLOT for j in range(TILES)]
PACK = 56
F32 = jnp.float32
BF16 = jnp.bfloat16
NT = (((1,), (1,)), ((), ()))
NN = (((1,), (0,)), ((), ()))


def dot(a, b, dims=NN):
    return lax.dot_general(a, b, dims, preferred_element_type=F32)


def split(x):
    hi = x.astype(BF16)
    return hi, (x - hi.astype(F32)).astype(BF16)


def onehot(mask):
    return jnp.where(mask, 1.0, 0.0).astype(BF16)


def rows_of(z_ref, first, j):
    return jnp.concatenate([z_ref[first + 2 * j : first + 2 * j + 1, :], z_ref[first + 2 * j + 1 : first + 2 * j + 2, :]], axis=1)


def main_kernel(slot_ref, z_ref, rel_ref, *refs):
    pieces = refs[:10]
    pk_ref, lg_ref, rg_ref = refs[10:13]
    hi_s, lo_s, lhs_s, rel_s, rhs_s, gl_s, gr_s, lhsb_s, rhsb_s, lhsr_s, rhsr_s, bias_s, rows_s, idx_s = refs[13:]

    for side in range(2):
        for k, (piece, places) in enumerate(zip(pieces[5 * side : 5 * side + 5], PLACES)):
            for i, place in enumerate(places):
                lanes = pl.ds(pl.multiple_of(slot_ref[16 * side + place] * R, R), R)
                hi, lo = split(piece[i])
                hi_s[:, lanes] = hi
                lo_s[:, lanes] = lo

    zt = jnp.concatenate([z_ref[W : W + PACK, :], jnp.zeros((R - PACK, R), F32)], axis=0).T
    lt_hi, lt_lo = split(z_ref[:W, :])
    sub_iota = lax.broadcasted_iota(jnp.int32, (SPREAD * R, TILE), 0).astype(F32)
    lane_iota = lax.broadcasted_iota(jnp.int32, (R, SPREAD * R), 1).astype(F32)
    rel_iota = lax.broadcasted_iota(jnp.int32, (R, TILE), 0)
    rel_iota = jnp.where(rel_iota < 48, rel_iota % 16, -1).astype(F32)

    rel3 = rel_ref[...]
    for j in range(TILES):
        c, at = divmod(j * TILE, CH)
        lanes = slice(at, at + TILE)
        base = FIRST[j] * R
        oh = onehot(sub_iota == rows_of(z_ref, W + 12, j) - float(base))
        cols = slice(base, base + SPREAD * R)
        rhs = dot(hi_s[:, cols], oh) + dot(lo_s[:, cols], oh)
        rhs_s[c, :, lanes] = rhs
        rhsb_s[c, :, lanes] = rhs.astype(BF16)
        ohr = jnp.concatenate(
            [onehot(lane_iota == zt[:, 12 + 2 * j + i : 13 + 2 * j + i] - float(base)) for i in range(2)], axis=0
        )
        rhsr_s[c, lanes, :] = dot(ohr, hi_s[:, cols], NT).astype(BF16)
        oh = onehot(sub_iota[:R] == rows_of(z_ref, W, j))
        lhs = dot(lt_hi, oh) + dot(lt_lo, oh)
        lhs_s[c, :, lanes] = lhs
        lhsb_s[c, :, lanes] = lhs.astype(BF16)
        ohr = jnp.concatenate([onehot(lane_iota[:, :R] == zt[:, 2 * j + i : 1 + 2 * j + i]) for i in range(2)], axis=0)
        lhsr_s[c, lanes, :] = dot(ohr, lt_hi, NT).astype(BF16)
        oh = onehot(rel_iota == rows_of(z_ref, W + 24, j))
        rel_s[c, :, lanes] = dot(rel3, oh)
        for i in range(2):
            live = jnp.broadcast_to(zt[:, 36 + 2 * j + i : 37 + 2 * j + i], (R, R))
            bias_s[c, at + i * R : at + (i + 1) * R, :] = jnp.where(live > 0.5, 0.0, -jnp.inf)
            named = jnp.broadcast_to(zt[:, 12 + 2 * j + i : 13 + 2 * j + i], (R, R))
            idx_s[j * TILE + i * R : j * TILE + (i + 1) * R, :] = named

    gl_s[...] = jnp.zeros_like(gl_s)
    gr_s[...] = jnp.zeros_like(gr_s)
    rel_grad = jnp.zeros((16, W), F32)
    neg_row = z_ref[W + 48 : W + 49, :]
    lane_row = lax.broadcasted_iota(jnp.int32, (1, R), 1)
    rel_rows = lax.broadcasted_iota(jnp.int32, (16, CH), 0).astype(F32)
    for c in range(SPANS):
        n = jnp.sum(jnp.where(lane_row == c, neg_row, 0.0)).astype(jnp.int32)
        lhs, rel, rhs = lhs_s[c], rel_s[c], rhs_s[c]
        left, right = lhs * rel, rhs * rel
        positive = jnp.sum(left * rhs, axis=0, keepdims=True)
        leftb, rightb = left.astype(BF16), right.astype(BF16)
        live = jnp.concatenate([rows_of(z_ref, W + 36, 2 * c), rows_of(z_ref, W + 36, 2 * c + 1)], axis=1)
        bias = jnp.concatenate([bias_s[n]] * 4, axis=1)

        def soft(neg_rows, edges):
            scores = dot(neg_rows, edges) + bias
            top = jnp.maximum(positive, jnp.max(scores, axis=0, keepdims=True))
            own = jnp.exp(positive - top)
            others = jnp.exp(scores - top)
            inv = 1.0 / (own + jnp.sum(others, axis=0, keepdims=True))
            return (others * (live * inv)).astype(BF16), own * inv

        tail_w, q_tail = soft(rhsr_s[n], leftb)
        head_w, q_head = soft(lhsr_s[n], rightb)
        weight = live * (q_tail + q_head - 2.0)
        grad_left = weight * rhs + dot(rhsb_s[n], tail_w)
        grad_right = dot(lhsb_s[n], head_w)
        gl_s[c] += grad_left * rel
        gr_s[c] += weight * left + grad_right * rel
        gr_s[n] += dot(leftb, tail_w, NT)
        gl_s[n] += dot(rightb, head_w, NT)
        ghi, glo = split(grad_left * lhs + grad_right * rhs)
        row = jnp.concatenate([rows_of(z_ref, W + 24, 2 * c), rows_of(z_ref, W + 24, 2 * c + 1)], axis=1)
        oh = onehot(rel_rows == row)
        rel_grad += dot(oh, ghi, NT) + dot(oh, glo, NT)
    tail = jnp.concatenate([rel_grad[:, 384:], jnp.zeros((16, R - 16), F32)], axis=1)
    rg_ref[...] = jnp.concatenate([rel_grad[:, :R], rel_grad[:, R : 2 * R], rel_grad[:, 2 * R : 3 * R], tail], axis=0)

    lg = jnp.zeros((W, R), F32)
    same = onehot(lax.broadcasted_iota(jnp.int32, (R, R), 0) == lax.broadcasted_iota(jnp.int32, (R, R), 1))
    for j in range(TILES):
        c, at = divmod(j * TILE, CH)
        lanes = slice(at, at + TILE)
        oh = onehot(sub_iota[:R] == rows_of(z_ref, W, j))
        hi, lo = split(gl_s[c, :, lanes])
        lg += dot(hi, oh, NT) + dot(lo, oh, NT)
        hi, lo = split(jnp.concatenate([gr_s[c, :, lanes], jnp.zeros((512 - W, TILE), F32)], axis=0))
        for i in range(2):
            at = j * TILE + i * R
            part = slice(i * R, (i + 1) * R)
            rows_s[at : at + R, :] = dot(same, hi[:, part], NT) + dot(same, lo[:, part], NT)
    lg_ref[...] = lg
    lane = lax.broadcasted_iota(jnp.int32, (8, R), 1)
    for o in range(N_SHARD):
        for k in range(3):
            pk_ref[o, k * SLOT : (k + 1) * SLOT, :] = rows_s[o * SLOT : (o + 1) * SLOT, k * R : (k + 1) * R]
        tail = jnp.zeros((8, R), F32)
        for k in range(SLOT // 8):
            at = slice(o * SLOT + 8 * k, o * SLOT + 8 * k + 8)
            piece = rows_s[at, 3 * R :]
            tail += piece if k == 0 else pltpu.roll(piece, 16 * k, 1)
            tail = jnp.where(lane == 96 + k, idx_s[at, :] - float(o * R), tail)
        pk_ref[o, 3 * SLOT :, :] = tail


PLACES = [(0, 1, 2, 3), (4, 5, 6, 7), (12, 13, 14, 15), (8, 9), (10, 11)]
BLOCK = 3 * SLOT + 8


def main_call(slots, z, rel, pieces):
    smem = pl.BlockSpec(memory_space=pltpu.SMEM)
    vmem = pl.BlockSpec(memory_space=pltpu.VMEM)
    big = pltpu.VMEM((SPANS, W, CH), F32)
    half = pltpu.VMEM((SPANS, W, CH), BF16)
    rows = pltpu.VMEM((SPANS, CH, W), BF16)
    return pl.pallas_call(
        main_kernel,
        out_shape=[jax.ShapeDtypeStruct((N_SHARD, BLOCK, R), F32), jax.ShapeDtypeStruct((W, R), F32), jax.ShapeDtypeStruct((64, R), F32)],
        in_specs=[smem] + [vmem] * 12,
        out_specs=[vmem] * 3,
        scratch_shapes=[
            pltpu.VMEM((W, N_SHARD * R), BF16),
            pltpu.VMEM((W, N_SHARD * R), BF16),
            big, big, big, big, big, half, half, rows, rows,
            pltpu.VMEM((SPANS, CH, R), F32),
            pltpu.VMEM((E, 512), F32),
            pltpu.VMEM((E, R), F32),
        ],
        compiler_params=pltpu.CompilerParams(vmem_limit_bytes=46 * 1024 * 1024),
        cost_estimate=pl.CostEstimate(flops=12_000_000_000, bytes_accessed=14_000_000, transcendentals=1_600_000),
        name="edges",
    )(slots, z, rel, *pieces)


def call(kernel, shapes, name):
    return pl.pallas_call(kernel, out_shape=[jax.ShapeDtypeStruct(v, F32) for v in shapes], name=name)


def pack_kernel(pos_ref, count_ref, neg_ref, table_ref, lhs_ref, rhs_ref, relidx_ref, relation_ref, z_ref, rel_ref, slot_ref):
    x, y, c = pos_ref[0], pos_ref[1], pos_ref[2]
    for side in range(2):
        core = c if side == 0 else 1 - c
        for place in range(16):
            jq, jp = divmod(place, 4)
            dx = jnp.where(core == 0, jp, jq)
            dy = jnp.where(core == 0, jq, jp)
            slot_ref[16 * side + place] = (((x + dx) & 3) * 4 + ((y + dy) & 3)) * 2 + core
    z_ref[:W, :] = table_ref[...]
    shape = (E // R, R)
    edge = lax.broadcasted_iota(jnp.int32, shape, 0) * R + lax.broadcasted_iota(jnp.int32, shape, 1)
    owner = jnp.zeros(shape, jnp.int32)
    live = jnp.zeros(shape, jnp.int32)
    for o in range(N_SHARD):
        inside = jnp.where(edge >= o * SLOT, 1, 0)
        owner = owner + inside
        live = live + inside * jnp.where(edge < o * SLOT + count_ref[0, o], 1, 0) * jnp.where(edge < (o + 1) * SLOT, 1, 0)
    z_ref[W : W + 12, :] = lhs_ref[...].astype(F32)
    z_ref[W + 12 : W + 24, :] = ((owner - 1) * R + rhs_ref[...]).astype(F32)
    z_ref[W + 24 : W + 36, :] = relidx_ref[...].astype(F32)
    z_ref[W + 36 : W + 48, :] = live.astype(F32)
    lane = lax.broadcasted_iota(jnp.int32, (PACK - 48, R), 1)
    neg = jnp.zeros((PACK - 48, R), jnp.int32)
    for c in range(SPANS):
        neg = jnp.where(lane == c, neg_ref[c], neg)
    z_ref[W + 48 :, :] = neg.astype(F32)
    rel = jnp.concatenate([relation_ref[...]] * 8, axis=0)
    rel = jnp.concatenate([rel, jnp.zeros((R, 512 - W), F32)], axis=1).T[:W]
    part = lax.broadcasted_iota(jnp.int32, (W, R), 1) // 16
    hi = rel.astype(BF16).astype(F32)
    mid = (rel - hi).astype(BF16).astype(F32)
    low = rel - hi - mid
    rel_ref[...] = jnp.where(part == 0, hi, jnp.where(part == 1, mid, jnp.where(part == 2, low, 0.0))).astype(BF16)


def pack_call(pos, count, neg, table, lhs, rhs, relidx, relation):
    smem = pl.BlockSpec(memory_space=pltpu.SMEM)
    vmem = pl.BlockSpec(memory_space=pltpu.VMEM)
    return pl.pallas_call(
        pack_kernel,
        out_shape=[
            jax.ShapeDtypeStruct((W + PACK, R), F32),
            jax.ShapeDtypeStruct((W, R), BF16),
            jax.ShapeDtypeStruct((2 * 16,), jnp.int32),
        ],
        in_specs=[smem] * 3 + [vmem] * 5,
        out_specs=[vmem, vmem, smem],
        name="pack",
    )(pos, count, neg, table, lhs, rhs, relidx, relation)


def last_kernel(pk_ref, lhs_ref, acc_ref, ent_ref, state_ref):
    tails = pk_ref[:, 3 * SLOT :, :].reshape(N_SHARD * 8, R)
    names = tails.T
    iota = lax.broadcasted_iota(jnp.int32, (R, N_SHARD * 8), 0).astype(F32)
    lane = lax.broadcasted_iota(jnp.int32, (N_SHARD * 8, R), 1)
    total = jnp.zeros((R, 512), F32)
    for k in range(SLOT // 8):
        oh = onehot(iota == names[96 + k : 97 + k, :])
        tail = tails if k == 0 else pltpu.roll(tails, R - 16 * k, 1)
        blocks = [pk_ref[:, b * SLOT + 8 * k : b * SLOT + 8 * k + 8, :].reshape(N_SHARD * 8, R) for b in range(3)]
        hi, lo = split(jnp.concatenate(blocks + [jnp.where(lane < 16, tail, 0.0)], axis=1))
        total += dot(oh, hi) + dot(oh, lo)
    g = total.T[:W] + lhs_ref[...]
    state_ref[...] = acc_ref[...] + jnp.sum(g * g, axis=0, keepdims=True) * (1.0 / W)
    ent_ref[...] = g


def step_pairs(first, second):
    pairs = []
    for s in range(N_SHARD):
        x, y, c = s // 8, (s // 2) % 4, s % 2
        dx, dy = (first, second) if c == 0 else (second, first)
        pairs.append((s, (((x + dx) % 4) * 4 + (y + dy) % 4) * 2 + c))
    return pairs


def move(value, first=0, second=0):
    return lax.ppermute(value, "shard", step_pairs(first, second))


def swap_core(value):
    return lax.ppermute(value, "shard", [(s, s ^ 1) for s in range(N_SHARD)])


def swap_dom(value, mask):
    return lax.ppermute(value, "dom", [(d, d ^ mask) for d in range(N_DOM)])


def pair_move(value, mask):
    return lax.switch(mask - 1, [functools.partial(swap_dom, mask=m) for m in range(1, N_DOM)], value)


def after(value, first):
    return value + jnp.minimum(jnp.abs(first), 0.0)


def gather_tables(t, payload, mask):
    x1 = jnp.stack([t, move(t, first=-1), move(t, first=2), move(t, first=1)])
    z = pair_move(after(payload, x1.reshape(-1, R)[: W + PACK]), mask)
    o1, o3 = move(x1, second=-1), move(x1, second=1)
    f2, g2 = move(after(o3[:2], z[:W]), second=1), move(after(o1[2:], z[:W]), second=-1)
    own = [x1, o1, o3, f2, g2]
    return z, own + [swap_core(v) for v in own]


def move_back(lhs, rel, mask):
    both = jnp.concatenate([lhs, rel])
    other = swap_dom(both, mask)
    rel = rel + other[W:]
    for more in {1: (2, 6), 2: (1, 6), 3: (1, 6)}.get(mask, (1, 2)):
        rel = rel + swap_dom(rel, more)
    return other[:W], rel


def sum_shard(value):
    for mask in (1, 2, 6, 8, 24):
        value = value + lax.ppermute(value, "shard", [(s, s ^ mask) for s in range(N_SHARD)])
    return value


def local(embedding, accumulator, relation, plan, lhs_index, rhs_index, rel_index, slot_count, neg_span):
    shard = lax.axis_index("shard")
    pos = jnp.stack([shard // 8, (shard // 2) % 4, shard % 2]).astype(jnp.int32)
    mask = plan[0]
    table = embedding.T
    rows = (E // R, R)
    payload, rel, slots = pack_call(
        pos, slot_count, neg_span, table, lhs_index.reshape(rows), rhs_index.reshape(rows), rel_index.reshape(rows), relation
    )
    z, pieces = gather_tables(table, payload, mask)
    packed, lhs_grad, rel_grad = main_call(slots, z, rel, pieces)
    returned = lax.all_to_all(packed, "shard", 0, 0, tiled=True)
    back = [functools.partial(move_back, mask=m) for m in range(1, N_DOM)]
    lhs_grad, rel_grad = lax.switch(mask - 1, back, lhs_grad, rel_grad)
    rel_grad = sum_shard(rel_grad)
    entity_grad, state = call(last_kernel, [(W, R), (1, R)], "last")(returned, lhs_grad, accumulator.reshape(1, R))
    relation_grad = jnp.concatenate([rel_grad[:16], rel_grad[16:32], rel_grad[32:48], rel_grad[48:, : W - 3 * R]], axis=1)
    return entity_grad.T, state.reshape(R), relation_grad


def solution(mesh):
    both = P(("dom", "shard"))
    rows = P(("dom", "shard"), None)
    in_specs = (rows, both, P(), P(), both, both, both, rows, both)
    return jax.shard_map(local, mesh=mesh, in_specs=in_specs, out_specs=(rows, both, P()), check_vma=False)
```

```python
import functools

import jax
import jax.numpy as jnp
from jax import lax
from jax.experimental import pallas as pl
from jax.experimental.pallas import tpu as pltpu
from jax.sharding import PartitionSpec as P

W = 400
R = 128
E = 1536
CH = 512
SLOT = 48
SPANS = 3
N_DOM = 8
N_SHARD = 32
TILE = 256
TILES = E // TILE
SPREAD = 6
FIRST = [TILE * j // SLOT for j in range(TILES)]
PACK = 56
F32 = jnp.float32
BF16 = jnp.bfloat16
NT = (((1,), (1,)), ((), ()))
NN = (((1,), (0,)), ((), ()))


def dot(a, b, dims=NN):
    return lax.dot_general(a, b, dims, preferred_element_type=F32)


def split(x):
    hi = x.astype(BF16)
    return hi, (x - hi.astype(F32)).astype(BF16)


def onehot(mask):
    return jnp.where(mask, 1.0, 0.0).astype(BF16)


def row_at(z_ref, first, index):
    return z_ref[pl.ds(first + index, 1), :]


def rows_of(z_ref, first, j, count=2):
    return jnp.concatenate([row_at(z_ref, first, count * j + i) for i in range(count)], axis=1)


def columns(row):
    return jnp.broadcast_to(row, (R, R)).T


def main_kernel(slot_ref, z_ref, rel_ref, *refs):
    pieces = refs[:10]
    pk_ref, lg_ref, rg_ref = refs[10:13]
    hi_s, lo_s, lhs_s, rel_s, rhs_s, gl_s, gr_s, lhsb_s, rhsb_s, lhsr_s, rhsr_s, bias_s, rows_s, idx_s, rel_acc = refs[13:]

    for side in range(2):
        for piece, places in zip(pieces[5 * side : 5 * side + 5], PLACES):

            def one_table(i, _, piece=piece, first=16 * side + places[0]):
                lanes = pl.ds(pl.multiple_of(slot_ref[first + i] * R, R), R)
                hi, lo = split(piece[i])
                hi_s[:, lanes] = hi
                lo_s[:, lanes] = lo
                return 0

            lax.fori_loop(0, len(places), one_table, 0, unroll=2)

    lt_hi, lt_lo = split(z_ref[:W, :])
    sub_iota = lax.broadcasted_iota(jnp.int32, (SPREAD * R, TILE), 0).astype(F32)
    pad = jnp.zeros((512 - W, TILE), F32)
    rel_iota = lax.broadcasted_iota(jnp.int32, (R, TILE), 0)
    rel_iota = jnp.where(rel_iota < 48, rel_iota % 16, -1).astype(F32)
    rel3 = rel_ref[...]

    def one_tile(j, _):
        c = j // 2
        at = pl.multiple_of((j % 2) * TILE, TILE)
        lanes = pl.ds(at, TILE)
        base = (j * TILE // SLOT) * R
        start = base.astype(F32)
        cols = pl.ds(pl.multiple_of(base, R), SPREAD * R)
        oh = onehot(sub_iota == rows_of(z_ref, W + 12, j) - start)
        hi = hi_s[:, cols]
        rhs = dot(hi, oh) + dot(lo_s[:, cols], oh)
        rhs_s[c, :, lanes] = rhs
        rhsb_s[c, :, lanes] = rhs.astype(BF16)
        named = [columns(row_at(z_ref, W + 12, 2 * j + i)) for i in range(2)]
        rhsr_s[c, lanes, :] = jnp.concatenate([rhs, pad], axis=0).T[:, :W].astype(BF16)
        idx_s[pl.ds(pl.multiple_of(j * TILE, TILE), TILE), :] = jnp.concatenate(named, axis=0)
        oh = onehot(sub_iota[:R] == rows_of(z_ref, W, j))
        lhs = dot(lt_hi, oh) + dot(lt_lo, oh)
        lhs_s[c, :, lanes] = lhs
        lhsb_s[c, :, lanes] = lhs.astype(BF16)
        lhsr_s[c, lanes, :] = jnp.concatenate([lhs, pad], axis=0).T[:, :W].astype(BF16)
        oh = onehot(rel_iota == rows_of(z_ref, W + 24, j))
        rel_s[c, :, lanes] = dot(rel3, oh)
        live = jnp.concatenate([columns(row_at(z_ref, W + 36, 2 * j + i)) for i in range(2)], axis=0)
        bias_s[c, lanes, :] = jnp.where(live > 0.5, 0.0, -jnp.inf)
        return 0

    lax.fori_loop(0, TILES, one_tile, 0, unroll=3)

    gl_s[...] = jnp.zeros_like(gl_s)
    gr_s[...] = jnp.zeros_like(gr_s)
    rel_acc[...] = jnp.zeros_like(rel_acc)
    neg_row = z_ref[W + 48 : W + 49, :]
    lane_row = lax.broadcasted_iota(jnp.int32, (1, R), 1)
    rel_rows = lax.broadcasted_iota(jnp.int32, (16, CH), 0).astype(F32)

    def one_block(c, _):
        n = jnp.sum(jnp.where(lane_row == c, neg_row, 0.0)).astype(jnp.int32)
        lhs, rel, rhs = lhs_s[c], rel_s[c], rhs_s[c]
        left, right = lhs * rel, rhs * rel
        positive = jnp.sum(left * rhs, axis=0, keepdims=True)
        leftb, rightb = left.astype(BF16), right.astype(BF16)
        live = rows_of(z_ref, W + 36, c, 4)
        bias = jnp.concatenate([bias_s[n]] * 4, axis=1)

        def soft(neg_rows, edges):
            scores = dot(neg_rows, edges) + bias
            top = jnp.maximum(positive, jnp.max(scores, axis=0, keepdims=True))
            own = jnp.exp(positive - top)
            others = jnp.exp(scores - top)
            inv = 1.0 / (own + jnp.sum(others, axis=0, keepdims=True))
            return (others * (live * inv)).astype(BF16), own * inv

        tail_w, q_tail = soft(rhsr_s[n], leftb)
        head_w, q_head = soft(lhsr_s[n], rightb)
        weight = live * (q_tail + q_head - 2.0)
        grad_left = weight * rhs + dot(rhsb_s[n], tail_w)
        grad_right = dot(lhsb_s[n], head_w)
        gl_s[c] += grad_left * rel
        gr_s[c] += weight * left + grad_right * rel
        gr_s[n] += dot(leftb, tail_w, NT)
        gl_s[n] += dot(rightb, head_w, NT)
        ghi, glo = split(grad_left * lhs + grad_right * rhs)
        oh = onehot(rel_rows == rows_of(z_ref, W + 24, c, 4))
        rel_acc[...] += dot(oh, ghi, NT) + dot(oh, glo, NT)
        return 0

    lax.fori_loop(0, SPANS, one_block, 0, unroll=1)
    rel_grad = rel_acc[...]
    tail = jnp.concatenate([rel_grad[:, 384:], jnp.zeros((16, R - 16), F32)], axis=1)
    rg_ref[...] = jnp.concatenate([rel_grad[:, :R], rel_grad[:, R : 2 * R], rel_grad[:, 2 * R : 3 * R], tail], axis=0)

    lg_ref[...] = jnp.zeros_like(lg_ref)

    def one_sum(j, _):
        c = j // 2
        lanes = pl.ds(pl.multiple_of((j % 2) * TILE, TILE), TILE)
        oh = onehot(sub_iota[:R] == rows_of(z_ref, W, j))
        hi, lo = split(gl_s[c, :, lanes])
        lg_ref[...] += dot(hi, oh, NT) + dot(lo, oh, NT)
        rows = pl.ds(pl.multiple_of(j * TILE, TILE), TILE)
        rows_s[rows, :] = jnp.concatenate([gr_s[c, :, lanes], pad], axis=0).T
        return 0

    lax.fori_loop(0, TILES, one_sum, 0, unroll=3)
    lane = lax.broadcasted_iota(jnp.int32, (8, R), 1)

    def one_slot(o, _):
        first = pl.multiple_of(o * SLOT, SLOT)
        for k in range(3):
            pk_ref[o, k * SLOT : (k + 1) * SLOT, :] = rows_s[pl.ds(first, SLOT), k * R : (k + 1) * R]
        tail = jnp.zeros((8, R), F32)
        base = (o * R).astype(F32)
        for k in range(SLOT // 8):
            at = pl.ds(pl.multiple_of(first + 8 * k, 8), 8)
            piece = rows_s[at, 3 * R :]
            tail += piece if k == 0 else pltpu.roll(piece, 16 * k, 1)
            tail = jnp.where(lane == 96 + k, idx_s[at, :] - base, tail)
        pk_ref[o, 3 * SLOT :, :] = tail
        return 0

    lax.fori_loop(0, N_SHARD, one_slot, 0, unroll=16)


PLACES = [(0, 1, 2, 3), (4, 5, 6, 7), (12, 13, 14, 15), (8, 9), (10, 11)]
BLOCK = 3 * SLOT + 8


def main_call(slots, z, rel, pieces):
    smem = pl.BlockSpec(memory_space=pltpu.SMEM)
    vmem = pl.BlockSpec(memory_space=pltpu.VMEM)
    big = pltpu.VMEM((SPANS, W, CH), F32)
    half = pltpu.VMEM((SPANS, W, CH), BF16)
    rows = pltpu.VMEM((SPANS, CH, W), BF16)
    return pl.pallas_call(
        main_kernel,
        out_shape=[jax.ShapeDtypeStruct((N_SHARD, BLOCK, R), F32), jax.ShapeDtypeStruct((W, R), F32), jax.ShapeDtypeStruct((64, R), F32)],
        in_specs=[smem] + [vmem] * 12,
        out_specs=[vmem] * 3,
        scratch_shapes=[
            pltpu.VMEM((W, N_SHARD * R), BF16),
            pltpu.VMEM((W, N_SHARD * R), BF16),
            big, big, big, big, big, half, half, rows, rows,
            pltpu.VMEM((SPANS, CH, R), F32),
            pltpu.VMEM((E, 512), F32),
            pltpu.VMEM((E, R), F32),
            pltpu.VMEM((16, W), F32),
        ],
        compiler_params=pltpu.CompilerParams(vmem_limit_bytes=46 * 1024 * 1024),
        cost_estimate=pl.CostEstimate(flops=12_000_000_000, bytes_accessed=14_000_000, transcendentals=1_600_000),
        name="edges",
    )(slots, z, rel, *pieces)


def call(kernel, shapes, name):
    return pl.pallas_call(kernel, out_shape=[jax.ShapeDtypeStruct(v, F32) for v in shapes], name=name)


def pack_kernel(pos_ref, count_ref, neg_ref, table_ref, lhs_ref, rhs_ref, relidx_ref, relation_ref, z_ref, rel_ref, slot_ref):
    x, y, c = pos_ref[0], pos_ref[1], pos_ref[2]
    for side in range(2):
        core = c if side == 0 else 1 - c
        for place in range(16):
            jq, jp = divmod(place, 4)
            dx = jnp.where(core == 0, jp, jq)
            dy = jnp.where(core == 0, jq, jp)
            slot_ref[16 * side + place] = (((x + dx) & 3) * 4 + ((y + dy) & 3)) * 2 + core
    z_ref[:W, :] = table_ref[...]
    shape = (E // R, R)
    edge = lax.broadcasted_iota(jnp.int32, shape, 0) * R + lax.broadcasted_iota(jnp.int32, shape, 1)
    owner = jnp.zeros(shape, jnp.int32)
    live = jnp.zeros(shape, jnp.int32)
    for o in range(N_SHARD):
        inside = jnp.where(edge >= o * SLOT, 1, 0)
        owner = owner + inside
        live = live + inside * jnp.where(edge < o * SLOT + count_ref[0, o], 1, 0) * jnp.where(edge < (o + 1) * SLOT, 1, 0)
    z_ref[W : W + 12, :] = lhs_ref[...].astype(F32)
    z_ref[W + 12 : W + 24, :] = ((owner - 1) * R + rhs_ref[...]).astype(F32)
    z_ref[W + 24 : W + 36, :] = relidx_ref[...].astype(F32)
    z_ref[W + 36 : W + 48, :] = live.astype(F32)
    lane = lax.broadcasted_iota(jnp.int32, (PACK - 48, R), 1)
    neg = jnp.zeros((PACK - 48, R), jnp.int32)
    for c in range(SPANS):
        neg = jnp.where(lane == c, neg_ref[c], neg)
    z_ref[W + 48 :, :] = neg.astype(F32)
    rel = jnp.concatenate([relation_ref[...]] * 8, axis=0)
    rel = jnp.concatenate([rel, jnp.zeros((R, 512 - W), F32)], axis=1).T[:W]
    part = lax.broadcasted_iota(jnp.int32, (W, R), 1) // 16
    hi = rel.astype(BF16).astype(F32)
    mid = (rel - hi).astype(BF16).astype(F32)
    low = rel - hi - mid
    rel_ref[...] = jnp.where(part == 0, hi, jnp.where(part == 1, mid, jnp.where(part == 2, low, 0.0))).astype(BF16)


def pack_call(pos, count, neg, table, lhs, rhs, relidx, relation):
    smem = pl.BlockSpec(memory_space=pltpu.SMEM)
    vmem = pl.BlockSpec(memory_space=pltpu.VMEM)
    return pl.pallas_call(
        pack_kernel,
        out_shape=[
            jax.ShapeDtypeStruct((W + PACK, R), F32),
            jax.ShapeDtypeStruct((W, R), BF16),
            jax.ShapeDtypeStruct((2 * 16,), jnp.int32),
        ],
        in_specs=[smem] * 3 + [vmem] * 5,
        out_specs=[vmem, vmem, smem],
        name="pack",
    )(pos, count, neg, table, lhs, rhs, relidx, relation)


def last_kernel(pk_ref, lhs_ref, acc_ref, ent_ref, state_ref):
    tails = pk_ref[:, 3 * SLOT :, :].reshape(N_SHARD * 8, R)
    names = tails.T
    iota = lax.broadcasted_iota(jnp.int32, (R, N_SHARD * 8), 0).astype(F32)
    lane = lax.broadcasted_iota(jnp.int32, (N_SHARD * 8, R), 1)
    total = jnp.zeros((R, 512), F32)
    for k in range(SLOT // 8):
        oh = onehot(iota == names[96 + k : 97 + k, :])
        tail = tails if k == 0 else pltpu.roll(tails, R - 16 * k, 1)
        blocks = [pk_ref[:, b * SLOT + 8 * k : b * SLOT + 8 * k + 8, :].reshape(N_SHARD * 8, R) for b in range(3)]
        hi, lo = split(jnp.concatenate(blocks + [jnp.where(lane < 16, tail, 0.0)], axis=1))
        total += dot(oh, hi) + dot(oh, lo)
    g = total.T[:W] + lhs_ref[...]
    state_ref[...] = acc_ref[...] + jnp.sum(g * g, axis=0, keepdims=True) * (1.0 / W)
    ent_ref[...] = g


def step_pairs(first, second):
    pairs = []
    for s in range(N_SHARD):
        x, y, c = s // 8, (s // 2) % 4, s % 2
        dx, dy = (first, second) if c == 0 else (second, first)
        pairs.append((s, (((x + dx) % 4) * 4 + (y + dy) % 4) * 2 + c))
    return pairs


def move(value, first=0, second=0):
    return lax.ppermute(value, "shard", step_pairs(first, second))


def swap_core(value):
    return lax.ppermute(value, "shard", [(s, s ^ 1) for s in range(N_SHARD)])


def swap_dom(value, mask):
    return lax.ppermute(value, "dom", [(d, d ^ mask) for d in range(N_DOM)])


def pair_move(value, mask):
    return lax.switch(mask - 1, [functools.partial(swap_dom, mask=m) for m in range(1, N_DOM)], value)


def after(value, first):
    return value + jnp.minimum(jnp.abs(first), 0.0)


def gather_tables(t, pack, mask):
    x1 = jnp.stack([t, move(t, first=-1), move(t, first=2), move(t, first=1)])
    payload, rel, slots = pack(x1[0])
    z = pair_move(payload, mask)
    o1, o3 = move(x1, second=-1), move(x1, second=1)
    f2, g2 = move(after(o3[:2], z[:W]), second=1), move(after(o1[2:], z[:W]), second=-1)
    own = [x1, o1, o3, f2, g2]
    return slots, z, rel, own + [swap_core(v) for v in own]


def sum_shard(value, masks):
    for mask in masks:
        value = value + lax.ppermute(value, "shard", [(s, s ^ mask) for s in range(N_SHARD)])
    return value


def move_back(lhs, rel, mask):
    other = swap_dom(jnp.concatenate([lhs, rel]), mask)
    rel = rel + other[W:]
    for step in {1: (2, 6), 2: (1, 6), 3: (1, 6)}.get(mask, (1, 2)):
        rel = rel + swap_dom(rel, step)
    return other[:W], rel


def local(embedding, accumulator, relation, plan, lhs_index, rhs_index, rel_index, slot_count, neg_span):
    shard = lax.axis_index("shard")
    pos = jnp.stack([shard // 8, (shard // 2) % 4, shard % 2]).astype(jnp.int32)
    mask = plan[0]
    table = embedding.T
    rows = (E // R, R)

    def pack(first):
        indices = [v.reshape(rows) for v in (lhs_index, rhs_index, rel_index)]
        return pack_call(pos, slot_count, neg_span, first, *indices, relation)

    slots, z, rel, pieces = gather_tables(table, pack, mask)
    packed, lhs_grad, rel_grad = main_call(slots, z, rel, pieces)
    returned = lax.all_to_all(packed, "shard", 0, 0, tiled=True)
    back = [functools.partial(move_back, mask=m) for m in range(1, N_DOM)]
    lhs_grad, rel_grad = lax.switch(mask - 1, back, lhs_grad, rel_grad)
    rel_grad = after(sum_shard(rel_grad, (1, 2, 6, 8)), returned[0, :64])
    entity_grad, state = call(last_kernel, [(W, R), (1, R)], "last")(returned, lhs_grad, accumulator.reshape(1, R))
    rel_grad = after(sum_shard(rel_grad, (24,)), entity_grad[:64])
    relation_grad = jnp.concatenate([rel_grad[:16], rel_grad[16:32], rel_grad[32:48], rel_grad[48:, : W - 3 * R]], axis=1)
    return entity_grad.T, state.reshape(R), relation_grad


def solution(mesh):
    both = P(("dom", "shard"))
    rows = P(("dom", "shard"), None)
    in_specs = (rows, both, P(), P(), both, both, both, rows, both)
    return jax.shard_map(local, mesh=mesh, in_specs=in_specs, out_specs=(rows, both, P()), check_vma=False)
```

```python
import functools

import jax
import jax.numpy as jnp
from jax import lax
from jax.experimental import pallas as pl
from jax.experimental.pallas import tpu as pltpu
from jax.sharding import PartitionSpec as P

W = 400
R = 128
E = 1536
CH = 512
SLOT = 48
SPANS = 3
N_DOM = 8
N_SHARD = 32
TILE = 256
TILES = E // TILE
SPREAD = 6
FIRST = [TILE * j // SLOT for j in range(TILES)]
PACK = 56
F32 = jnp.float32
BF16 = jnp.bfloat16
NT = (((1,), (1,)), ((), ()))
NN = (((1,), (0,)), ((), ()))


def dot(a, b, dims=NN):
    return lax.dot_general(a, b, dims, preferred_element_type=F32)


def split(x):
    hi = x.astype(BF16)
    return hi, (x - hi.astype(F32)).astype(BF16)


def onehot(mask):
    return jnp.where(mask, 1.0, 0.0).astype(BF16)


def row_at(z_ref, first, index):
    return z_ref[pl.ds(first + index, 1), :]


def rows_of(z_ref, first, j, count=2):
    return jnp.concatenate([row_at(z_ref, first, count * j + i) for i in range(count)], axis=1)


def columns(row):
    return jnp.broadcast_to(row, (R, R)).T


def main_kernel(slot_ref, z_ref, rel_ref, *refs):
    pieces = refs[:10]
    pk_ref, lg_ref, rg_ref = refs[10:13]
    hi_s, lo_s, lhs_s, rel_s, rhs_s, gl_s, gr_s, lhsb_s, rhsb_s, lhsr_s, rhsr_s, bias_s, rows_s, idx_s, rel_acc = refs[13:]

    for side in range(2):
        for piece, places in zip(pieces[5 * side : 5 * side + 5], PLACES):

            def one_table(i, _, piece=piece, first=16 * side + places[0]):
                lanes = pl.ds(pl.multiple_of(slot_ref[first + i] * R, R), R)
                hi, lo = split(piece[i])
                hi_s[:, lanes] = hi
                lo_s[:, lanes] = lo
                return 0

            lax.fori_loop(0, len(places), one_table, 0, unroll=2)

    lt_hi, lt_lo = split(z_ref[:W, :])
    sub_iota = lax.broadcasted_iota(jnp.int32, (SPREAD * R, TILE), 0).astype(F32)
    pad = jnp.zeros((512 - W, TILE), F32)
    rel_iota = lax.broadcasted_iota(jnp.int32, (R, TILE), 0)
    rel_iota = jnp.where(rel_iota < 48, rel_iota % 16, -1).astype(F32)
    rel3 = rel_ref[...]

    def one_tile(j, _):
        c = j // 2
        at = pl.multiple_of((j % 2) * TILE, TILE)
        lanes = pl.ds(at, TILE)
        base = (j * TILE // SLOT) * R
        start = base.astype(F32)
        cols = pl.ds(pl.multiple_of(base, R), SPREAD * R)
        oh = onehot(sub_iota == rows_of(z_ref, W + 12, j) - start)
        hi = hi_s[:, cols]
        rhs = dot(hi, oh) + dot(lo_s[:, cols], oh)
        rhs_s[c, :, lanes] = rhs
        rhsb_s[c, :, lanes] = rhs.astype(BF16)
        named = [columns(row_at(z_ref, W + 12, 2 * j + i)) for i in range(2)]
        rhsr_s[c, lanes, :] = jnp.concatenate([rhs, pad], axis=0).T[:, :W].astype(BF16)
        idx_s[pl.ds(pl.multiple_of(j * TILE, TILE), TILE), :] = jnp.concatenate(named, axis=0)
        oh = onehot(sub_iota[:R] == rows_of(z_ref, W, j))
        lhs = dot(lt_hi, oh) + dot(lt_lo, oh)
        lhs_s[c, :, lanes] = lhs
        lhsb_s[c, :, lanes] = lhs.astype(BF16)
        lhsr_s[c, lanes, :] = jnp.concatenate([lhs, pad], axis=0).T[:, :W].astype(BF16)
        oh = onehot(rel_iota == rows_of(z_ref, W + 24, j))
        rel_s[c, :, lanes] = dot(rel3, oh)
        live = jnp.concatenate([columns(row_at(z_ref, W + 36, 2 * j + i)) for i in range(2)], axis=0)
        bias_s[c, lanes, :] = jnp.where(live > 0.5, 0.0, -jnp.inf)
        return 0

    lax.fori_loop(0, TILES, one_tile, 0, unroll=3)

    gl_s[...] = jnp.zeros_like(gl_s)
    gr_s[...] = jnp.zeros_like(gr_s)
    rel_acc[...] = jnp.zeros_like(rel_acc)
    neg_row = z_ref[W + 48 : W + 49, :]
    lane_row = lax.broadcasted_iota(jnp.int32, (1, R), 1)
    rel_rows = lax.broadcasted_iota(jnp.int32, (16, CH), 0).astype(F32)

    def one_block(c, _):
        n = jnp.sum(jnp.where(lane_row == c, neg_row, 0.0)).astype(jnp.int32)
        lhs, rel, rhs = lhs_s[c], rel_s[c], rhs_s[c]
        left, right = lhs * rel, rhs * rel
        positive = jnp.sum(left * rhs, axis=0, keepdims=True)
        leftb, rightb = left.astype(BF16), right.astype(BF16)
        live = rows_of(z_ref, W + 36, c, 4)
        bias = jnp.concatenate([bias_s[n]] * 4, axis=1)

        def soft(neg_rows, edges):
            scores = dot(neg_rows, edges) + bias
            top = jnp.maximum(positive, jnp.max(scores, axis=0, keepdims=True))
            own = jnp.exp(positive - top)
            others = jnp.exp(scores - top)
            inv = 1.0 / (own + jnp.sum(others, axis=0, keepdims=True))
            return (others * (live * inv)).astype(BF16), own * inv

        tail_w, q_tail = soft(rhsr_s[n], leftb)
        head_w, q_head = soft(lhsr_s[n], rightb)
        weight = live * (q_tail + q_head - 2.0)
        grad_left = weight * rhs + dot(rhsb_s[n], tail_w)
        grad_right = dot(lhsb_s[n], head_w)
        gl_s[c] += grad_left * rel
        gr_s[c] += weight * left + grad_right * rel
        gr_s[n] += dot(leftb, tail_w, NT)
        gl_s[n] += dot(rightb, head_w, NT)
        ghi, glo = split(grad_left * lhs + grad_right * rhs)
        oh = onehot(rel_rows == rows_of(z_ref, W + 24, c, 4))
        rel_acc[...] += dot(oh, ghi, NT) + dot(oh, glo, NT)
        return 0

    lax.fori_loop(0, SPANS, one_block, 0, unroll=1)
    rel_grad = rel_acc[...]
    tail = jnp.concatenate([rel_grad[:, 384:], jnp.zeros((16, R - 16), F32)], axis=1)
    rg_ref[...] = jnp.concatenate([rel_grad[:, :R], rel_grad[:, R : 2 * R], rel_grad[:, 2 * R : 3 * R], tail], axis=0)

    lg_ref[...] = jnp.zeros_like(lg_ref)

    def one_sum(j, _):
        c = j // 2
        lanes = pl.ds(pl.multiple_of((j % 2) * TILE, TILE), TILE)
        oh = onehot(sub_iota[:R] == rows_of(z_ref, W, j))
        hi, lo = split(gl_s[c, :, lanes])
        lg_ref[...] += dot(hi, oh, NT) + dot(lo, oh, NT)
        rows = pl.ds(pl.multiple_of(j * TILE, TILE), TILE)
        rows_s[rows, :] = jnp.concatenate([gr_s[c, :, lanes], pad], axis=0).T
        return 0

    lax.fori_loop(0, TILES, one_sum, 0, unroll=3)
    lane = lax.broadcasted_iota(jnp.int32, (8, R), 1)

    def one_slot(o, _):
        first = pl.multiple_of(o * SLOT, SLOT)
        for k in range(3):
            pk_ref[o, k * SLOT : (k + 1) * SLOT, :] = rows_s[pl.ds(first, SLOT), k * R : (k + 1) * R]
        tail = jnp.zeros((8, R), F32)
        base = (o * R).astype(F32)
        for k in range(SLOT // 8):
            at = pl.ds(pl.multiple_of(first + 8 * k, 8), 8)
            piece = rows_s[at, 3 * R :]
            tail += piece if k == 0 else pltpu.roll(piece, 16 * k, 1)
            tail = jnp.where(lane == 96 + k, idx_s[at, :] - base, tail)
        pk_ref[o, 3 * SLOT :, :] = tail
        return 0

    lax.fori_loop(0, N_SHARD, one_slot, 0, unroll=16)


PLACES = [(0, 1, 2, 3), (4, 5, 6, 7), (12, 13, 14, 15), (8, 9), (10, 11)]
BLOCK = 3 * SLOT + 8


def main_call(slots, z, rel, pieces):
    smem = pl.BlockSpec(memory_space=pltpu.SMEM)
    vmem = pl.BlockSpec(memory_space=pltpu.VMEM)
    big = pltpu.VMEM((SPANS, W, CH), F32)
    half = pltpu.VMEM((SPANS, W, CH), BF16)
    rows = pltpu.VMEM((SPANS, CH, W), BF16)
    return pl.pallas_call(
        main_kernel,
        out_shape=[jax.ShapeDtypeStruct((N_SHARD, BLOCK, R), F32), jax.ShapeDtypeStruct((W, R), F32), jax.ShapeDtypeStruct((64, R), F32)],
        in_specs=[smem] + [vmem] * 12,
        out_specs=[vmem] * 3,
        scratch_shapes=[
            pltpu.VMEM((W, N_SHARD * R), BF16),
            pltpu.VMEM((W, N_SHARD * R), BF16),
            big, big, big, big, big, half, half, rows, rows,
            pltpu.VMEM((SPANS, CH, R), F32),
            pltpu.VMEM((E, 512), F32),
            pltpu.VMEM((E, R), F32),
            pltpu.VMEM((16, W), F32),
        ],
        compiler_params=pltpu.CompilerParams(vmem_limit_bytes=46 * 1024 * 1024),
        cost_estimate=pl.CostEstimate(flops=12_000_000_000, bytes_accessed=14_000_000, transcendentals=1_600_000),
        name="edges",
    )(slots, z, rel, *pieces)


def call(kernel, shapes, name):
    return pl.pallas_call(kernel, out_shape=[jax.ShapeDtypeStruct(v, F32) for v in shapes], name=name)


def pack_kernel(pos_ref, count_ref, neg_ref, table_ref, lhs_ref, rhs_ref, relidx_ref, relation_ref, z_ref, rel_ref, slot_ref):
    x, y, c = pos_ref[0], pos_ref[1], pos_ref[2]
    for side in range(2):
        core = c if side == 0 else 1 - c
        for place in range(16):
            jq, jp = divmod(place, 4)
            dx = jnp.where(core == 0, jp, jq)
            dy = jnp.where(core == 0, jq, jp)
            slot_ref[16 * side + place] = (((x + dx) & 3) * 4 + ((y + dy) & 3)) * 2 + core
    z_ref[:W, :] = table_ref[...]
    shape = (E // R, R)
    edge = lax.broadcasted_iota(jnp.int32, shape, 0) * R + lax.broadcasted_iota(jnp.int32, shape, 1)
    owner = jnp.zeros(shape, jnp.int32)
    live = jnp.zeros(shape, jnp.int32)
    for o in range(N_SHARD):
        inside = jnp.where(edge >= o * SLOT, 1, 0)
        owner = owner + inside
        live = live + inside * jnp.where(edge < o * SLOT + count_ref[0, o], 1, 0) * jnp.where(edge < (o + 1) * SLOT, 1, 0)
    z_ref[W : W + 12, :] = lhs_ref[...].astype(F32)
    z_ref[W + 12 : W + 24, :] = ((owner - 1) * R + rhs_ref[...]).astype(F32)
    z_ref[W + 24 : W + 36, :] = relidx_ref[...].astype(F32)
    z_ref[W + 36 : W + 48, :] = live.astype(F32)
    lane = lax.broadcasted_iota(jnp.int32, (PACK - 48, R), 1)
    neg = jnp.zeros((PACK - 48, R), jnp.int32)
    for c in range(SPANS):
        neg = jnp.where(lane == c, neg_ref[c], neg)
    z_ref[W + 48 :, :] = neg.astype(F32)
    rel = jnp.concatenate([relation_ref[...]] * 8, axis=0)
    rel = jnp.concatenate([rel, jnp.zeros((R, 512 - W), F32)], axis=1).T[:W]
    part = lax.broadcasted_iota(jnp.int32, (W, R), 1) // 16
    hi = rel.astype(BF16).astype(F32)
    mid = (rel - hi).astype(BF16).astype(F32)
    low = rel - hi - mid
    rel_ref[...] = jnp.where(part == 0, hi, jnp.where(part == 1, mid, jnp.where(part == 2, low, 0.0))).astype(BF16)


def pack_call(pos, count, neg, table, lhs, rhs, relidx, relation):
    smem = pl.BlockSpec(memory_space=pltpu.SMEM)
    vmem = pl.BlockSpec(memory_space=pltpu.VMEM)
    return pl.pallas_call(
        pack_kernel,
        out_shape=[
            jax.ShapeDtypeStruct((W + PACK, R), F32),
            jax.ShapeDtypeStruct((W, R), BF16),
            jax.ShapeDtypeStruct((2 * 16,), jnp.int32),
        ],
        in_specs=[smem] * 3 + [vmem] * 5,
        out_specs=[vmem, vmem, smem],
        name="pack",
    )(pos, count, neg, table, lhs, rhs, relidx, relation)


def last_kernel(pk_ref, lhs_ref, acc_ref, ent_ref, state_ref):
    tails = pk_ref[:, 3 * SLOT :, :].reshape(N_SHARD * 8, R)
    names = tails.T
    iota = lax.broadcasted_iota(jnp.int32, (R, N_SHARD * 8), 0).astype(F32)
    lane = lax.broadcasted_iota(jnp.int32, (N_SHARD * 8, R), 1)
    total = jnp.zeros((R, 512), F32)
    for k in range(SLOT // 8):
        oh = onehot(iota == names[96 + k : 97 + k, :])
        tail = tails if k == 0 else pltpu.roll(tails, R - 16 * k, 1)
        blocks = [pk_ref[:, b * SLOT + 8 * k : b * SLOT + 8 * k + 8, :].reshape(N_SHARD * 8, R) for b in range(3)]
        hi, lo = split(jnp.concatenate(blocks + [jnp.where(lane < 16, tail, 0.0)], axis=1))
        total += dot(oh, hi) + dot(oh, lo)
    g = total.T[:W] + lhs_ref[:W, :]
    state_ref[...] = acc_ref[...] + jnp.sum(g * g, axis=0, keepdims=True) * (1.0 / W)
    ent_ref[...] = g


def step_pairs(first, second):
    pairs = []
    for s in range(N_SHARD):
        x, y, c = s // 8, (s // 2) % 4, s % 2
        dx, dy = (first, second) if c == 0 else (second, first)
        pairs.append((s, (((x + dx) % 4) * 4 + (y + dy) % 4) * 2 + c))
    return pairs


def move(value, first=0, second=0):
    return lax.ppermute(value, "shard", step_pairs(first, second))


def swap_core(value):
    return lax.ppermute(value, "shard", [(s, s ^ 1) for s in range(N_SHARD)])


def swap_dom(value, mask):
    return lax.ppermute(value, "dom", [(d, d ^ mask) for d in range(N_DOM)])


def pair_move(value, mask):
    return lax.switch(mask - 1, [functools.partial(swap_dom, mask=m) for m in range(1, N_DOM)], value)


def after(value, first):
    return value + jnp.minimum(jnp.abs(first), 0.0)


def gather_tables(t, pack, mask):
    payload, rel, slots = pack(t)
    x1 = jnp.stack([payload[:W], move(t, first=-1), move(t, first=2), move(t, first=1)])
    z = pair_move(payload, mask)
    o1, o3 = move(x1, second=-1), move(x1, second=1)
    f2, g2 = move(after(o3[:2], z[:W]), second=1), move(after(o1[2:], z[:W]), second=-1)
    own = [x1, o1, o3, f2, g2]
    return slots, z, rel, own + [swap_core(v) for v in own]


def sum_shard(value, masks):
    for mask in masks:
        value = value + lax.ppermute(value, "shard", [(s, s ^ mask) for s in range(N_SHARD)])
    return value


def move_back(lhs, rel, mask):
    other = swap_dom(jnp.concatenate([lhs, rel]), mask)
    rel = rel + other[W:]
    for step in {1: (2, 6), 2: (1, 6), 3: (1, 6)}.get(mask, (1, 2)):
        rel = rel + swap_dom(rel, step)
    return other, rel


def local(embedding, accumulator, relation, plan, lhs_index, rhs_index, rel_index, slot_count, neg_span):
    shard = lax.axis_index("shard")
    pos = jnp.stack([shard // 8, (shard // 2) % 4, shard % 2]).astype(jnp.int32)
    mask = plan[0]
    table = embedding.T
    rows = (E // R, R)

    def pack(first):
        indices = [v.reshape(rows) for v in (lhs_index, rhs_index, rel_index)]
        return pack_call(pos, slot_count, neg_span, first, *indices, relation)

    slots, z, rel, pieces = gather_tables(table, pack, mask)
    packed, lhs_grad, rel_grad = main_call(slots, z, rel, pieces)
    returned = lax.all_to_all(packed, "shard", 0, 0, tiled=True)
    back = [functools.partial(move_back, mask=m) for m in range(1, N_DOM)]
    lhs_grad, rel_grad = lax.switch(mask - 1, back, lhs_grad, rel_grad)
    rel_grad = after(sum_shard(rel_grad, (1, 2, 6, 8)), returned[0, :64])
    entity_grad, state = call(last_kernel, [(W, R), (1, R)], "last")(returned, lhs_grad, accumulator.reshape(1, R))
    rel_grad = after(sum_shard(rel_grad, (24,)), entity_grad[:64])
    relation_grad = jnp.concatenate([rel_grad[:16], rel_grad[16:32], rel_grad[32:48], rel_grad[48:, : W - 3 * R]], axis=1)
    return entity_grad.T, state.reshape(R), relation_grad


def solution(mesh):
    both = P(("dom", "shard"))
    rows = P(("dom", "shard"), None)
    in_specs = (rows, both, P(), P(), both, both, both, rows, both)
    return jax.shard_map(local, mesh=mesh, in_specs=in_specs, out_specs=(rows, both, P()), check_vma=False)
```

```python
import functools

import jax
import jax.numpy as jnp
from jax import lax
from jax.experimental import pallas as pl
from jax.experimental.pallas import tpu as pltpu
from jax.sharding import PartitionSpec as P

W = 400
R = 128
E = 1536
CH = 512
SLOT = 48
SPANS = 3
N_DOM = 8
N_SHARD = 32
TILE = 256
TILES = E // TILE
SPREAD = 6
FIRST = [TILE * j // SLOT for j in range(TILES)]
PACK = 56
F32 = jnp.float32
BF16 = jnp.bfloat16
NT = (((1,), (1,)), ((), ()))
NN = (((1,), (0,)), ((), ()))


def dot(a, b, dims=NN):
    return lax.dot_general(a, b, dims, preferred_element_type=F32)


def split(x):
    hi = x.astype(BF16)
    return hi, (x - hi.astype(F32)).astype(BF16)


def onehot(mask):
    return jnp.where(mask, 1.0, 0.0).astype(BF16)


def row_at(z_ref, first, index):
    return z_ref[pl.ds(first + index, 1), :]


def rows_of(z_ref, first, j, count=2):
    return jnp.concatenate([row_at(z_ref, first, count * j + i) for i in range(count)], axis=1)


def columns(row):
    return jnp.broadcast_to(row, (R, R)).T


def main_kernel(slot_ref, z_ref, rel_ref, *refs):
    pieces = refs[:10]
    pk_ref, lg_ref, rg_ref = refs[10:13]
    hi_s, lo_s, lhs_s, rel_s, rhs_s, gl_s, gr_s, lhsb_s, rhsb_s, lhsr_s, rhsr_s, bias_s, rows_s, idx_s, rel_acc = refs[13:]

    for side in range(2):
        for piece, places in zip(pieces[5 * side : 5 * side + 5], PLACES):

            def one_table(i, _, piece=piece, first=16 * side + places[0]):
                lanes = pl.ds(pl.multiple_of(slot_ref[first + i] * R, R), R)
                hi, lo = split(piece[i])
                hi_s[:, lanes] = hi
                lo_s[:, lanes] = lo
                return 0

            lax.fori_loop(0, len(places), one_table, 0, unroll=2)

    lt_hi, lt_lo = split(z_ref[:W, :])
    sub_iota = lax.broadcasted_iota(jnp.int32, (SPREAD * R, TILE), 0).astype(F32)
    pad = jnp.zeros((512 - W, TILE), F32)
    rel_iota = lax.broadcasted_iota(jnp.int32, (R, TILE), 0)
    rel_iota = jnp.where(rel_iota < 48, rel_iota % 16, -1).astype(F32)
    rel3 = rel_ref[...]

    def one_tile(j, _):
        c = j // 2
        at = pl.multiple_of((j % 2) * TILE, TILE)
        lanes = pl.ds(at, TILE)
        base = (j * TILE // SLOT) * R
        start = base.astype(F32)
        cols = pl.ds(pl.multiple_of(base, R), SPREAD * R)
        oh = onehot(sub_iota == rows_of(z_ref, W + 12, j) - start)
        hi = hi_s[:, cols]
        rhs = dot(hi, oh) + dot(lo_s[:, cols], oh)
        rhs_s[c, :, lanes] = rhs
        rhsb_s[c, :, lanes] = rhs.astype(BF16)
        named = [columns(row_at(z_ref, W + 12, 2 * j + i)) for i in range(2)]
        rhsr_s[c, lanes, :] = jnp.concatenate([rhs, pad], axis=0).T[:, :W].astype(BF16)
        idx_s[pl.ds(pl.multiple_of(j * TILE, TILE), TILE), :] = jnp.concatenate(named, axis=0)
        oh = onehot(sub_iota[:R] == rows_of(z_ref, W, j))
        lhs = dot(lt_hi, oh) + dot(lt_lo, oh)
        lhs_s[c, :, lanes] = lhs
        lhsb_s[c, :, lanes] = lhs.astype(BF16)
        lhsr_s[c, lanes, :] = jnp.concatenate([lhs, pad], axis=0).T[:, :W].astype(BF16)
        oh = onehot(rel_iota == rows_of(z_ref, W + 24, j))
        rel_s[c, :, lanes] = dot(rel3, oh)
        live = jnp.concatenate([columns(row_at(z_ref, W + 36, 2 * j + i)) for i in range(2)], axis=0)
        bias_s[c, lanes, :] = jnp.where(live > 0.5, 0.0, -jnp.inf)
        return 0

    lax.fori_loop(0, TILES, one_tile, 0, unroll=3)

    gl_s[...] = jnp.zeros_like(gl_s)
    gr_s[...] = jnp.zeros_like(gr_s)
    rel_acc[...] = jnp.zeros_like(rel_acc)
    neg_row = z_ref[W + 48 : W + 49, :]
    lane_row = lax.broadcasted_iota(jnp.int32, (1, R), 1)
    rel_rows = lax.broadcasted_iota(jnp.int32, (16, CH), 0).astype(F32)

    def one_block(c, _):
        n = jnp.sum(jnp.where(lane_row == c, neg_row, 0.0)).astype(jnp.int32)
        lhs, rel, rhs = lhs_s[c], rel_s[c], rhs_s[c]
        left, right = lhs * rel, rhs * rel
        positive = jnp.sum(left * rhs, axis=0, keepdims=True)
        leftb, rightb = left.astype(BF16), right.astype(BF16)
        live = rows_of(z_ref, W + 36, c, 4)
        bias = jnp.concatenate([bias_s[n]] * 4, axis=1)

        def soft(neg_rows, edges):
            scores = dot(neg_rows, edges) + bias
            top = jnp.maximum(positive, jnp.max(scores, axis=0, keepdims=True))
            own = jnp.exp(positive - top)
            others = jnp.exp(scores - top)
            inv = 1.0 / (own + jnp.sum(others, axis=0, keepdims=True))
            return (others * (live * inv)).astype(BF16), own * inv

        tail_w, q_tail = soft(rhsr_s[n], leftb)
        head_w, q_head = soft(lhsr_s[n], rightb)
        weight = live * (q_tail + q_head - 2.0)
        grad_left = weight * rhs + dot(rhsb_s[n], tail_w)
        grad_right = dot(lhsb_s[n], head_w)
        gl_s[c] += grad_left * rel
        gr_s[c] += weight * left + grad_right * rel
        gr_s[n] += dot(leftb, tail_w, NT)
        gl_s[n] += dot(rightb, head_w, NT)
        ghi, glo = split(grad_left * lhs + grad_right * rhs)
        oh = onehot(rel_rows == rows_of(z_ref, W + 24, c, 4))
        rel_acc[...] += dot(oh, ghi, NT) + dot(oh, glo, NT)
        return 0

    lax.fori_loop(0, SPANS, one_block, 0, unroll=1)
    rel_grad = rel_acc[...]
    tail = jnp.concatenate([rel_grad[:, 384:], jnp.zeros((16, R - 16), F32)], axis=1)
    rg_ref[...] = jnp.concatenate([rel_grad[:, :R], rel_grad[:, R : 2 * R], rel_grad[:, 2 * R : 3 * R], tail], axis=0)

    lg_ref[...] = jnp.zeros_like(lg_ref)

    def one_sum(j, _):
        c = j // 2
        lanes = pl.ds(pl.multiple_of((j % 2) * TILE, TILE), TILE)
        oh = onehot(sub_iota[:R] == rows_of(z_ref, W, j))
        hi, lo = split(gl_s[c, :, lanes])
        lg_ref[...] += dot(hi, oh, NT) + dot(lo, oh, NT)
        rows = pl.ds(pl.multiple_of(j * TILE, TILE), TILE)
        rows_s[rows, :] = jnp.concatenate([gr_s[c, :, lanes], pad], axis=0).T
        return 0

    lax.fori_loop(0, TILES, one_sum, 0, unroll=3)
    lane = lax.broadcasted_iota(jnp.int32, (8, R), 1)

    def one_slot(o, _):
        first = pl.multiple_of(o * SLOT, SLOT)
        for k in range(3):
            pk_ref[o, k * SLOT : (k + 1) * SLOT, :] = rows_s[pl.ds(first, SLOT), k * R : (k + 1) * R]
        tail = jnp.zeros((8, R), F32)
        base = (o * R).astype(F32)
        for k in range(SLOT // 8):
            at = pl.ds(pl.multiple_of(first + 8 * k, 8), 8)
            piece = rows_s[at, 3 * R :]
            tail += piece if k == 0 else pltpu.roll(piece, 16 * k, 1)
            tail = jnp.where(lane == 96 + k, idx_s[at, :] - base, tail)
        pk_ref[o, 3 * SLOT :, :] = tail
        return 0

    lax.fori_loop(0, N_SHARD, one_slot, 0, unroll=16)


PLACES = [(0, 1, 2, 3), (4, 5, 6, 7), (12, 13, 14, 15), (8, 9), (10, 11)]
BLOCK = 3 * SLOT + 8


def main_call(slots, z, rel, pieces):
    smem = pl.BlockSpec(memory_space=pltpu.SMEM)
    vmem = pl.BlockSpec(memory_space=pltpu.VMEM)
    big = pltpu.VMEM((SPANS, W, CH), F32)
    half = pltpu.VMEM((SPANS, W, CH), BF16)
    rows = pltpu.VMEM((SPANS, CH, W), BF16)
    return pl.pallas_call(
        main_kernel,
        out_shape=[jax.ShapeDtypeStruct((N_SHARD, BLOCK, R), F32), jax.ShapeDtypeStruct((W, R), F32), jax.ShapeDtypeStruct((64, R), F32)],
        in_specs=[smem] + [vmem] * 12,
        out_specs=[vmem] * 3,
        scratch_shapes=[
            pltpu.VMEM((W, N_SHARD * R), BF16),
            pltpu.VMEM((W, N_SHARD * R), BF16),
            big, big, big, big, big, half, half, rows, rows,
            pltpu.VMEM((SPANS, CH, R), F32),
            pltpu.VMEM((E, 512), F32),
            pltpu.VMEM((E, R), F32),
            pltpu.VMEM((16, W), F32),
        ],
        compiler_params=pltpu.CompilerParams(vmem_limit_bytes=46 * 1024 * 1024),
        cost_estimate=pl.CostEstimate(flops=12_000_000_000, bytes_accessed=14_000_000, transcendentals=1_600_000),
        name="edges",
    )(slots, z, rel, *pieces)


def call(kernel, shapes, name):
    return pl.pallas_call(kernel, out_shape=[jax.ShapeDtypeStruct(v, F32) for v in shapes], name=name)


def pack_kernel(pos_ref, count_ref, neg_ref, table_ref, lhs_ref, rhs_ref, relidx_ref, relation_ref, z_ref, rel_ref, slot_ref):
    x, y, c = pos_ref[0], pos_ref[1], pos_ref[2]
    for side in range(2):
        core = c if side == 0 else 1 - c
        for place in range(16):
            jq, jp = divmod(place, 4)
            dx = jnp.where(core == 0, jp, jq)
            dy = jnp.where(core == 0, jq, jp)
            slot_ref[16 * side + place] = (((x + dx) & 3) * 4 + ((y + dy) & 3)) * 2 + core
    z_ref[:W, :] = table_ref[...]
    shape = (E // R, R)
    edge = lax.broadcasted_iota(jnp.int32, shape, 0) * R + lax.broadcasted_iota(jnp.int32, shape, 1)
    owner = jnp.zeros(shape, jnp.int32)
    live = jnp.zeros(shape, jnp.int32)
    for o in range(N_SHARD):
        inside = jnp.where(edge >= o * SLOT, 1, 0)
        owner = owner + inside
        live = live + inside * jnp.where(edge < o * SLOT + count_ref[0, o], 1, 0) * jnp.where(edge < (o + 1) * SLOT, 1, 0)
    z_ref[W : W + 12, :] = lhs_ref[...].astype(F32)
    z_ref[W + 12 : W + 24, :] = ((owner - 1) * R + rhs_ref[...]).astype(F32)
    z_ref[W + 24 : W + 36, :] = relidx_ref[...].astype(F32)
    z_ref[W + 36 : W + 48, :] = live.astype(F32)
    lane = lax.broadcasted_iota(jnp.int32, (PACK - 48, R), 1)
    neg = jnp.zeros((PACK - 48, R), jnp.int32)
    for c in range(SPANS):
        neg = jnp.where(lane == c, neg_ref[c], neg)
    z_ref[W + 48 :, :] = neg.astype(F32)
    rel = jnp.concatenate([relation_ref[...]] * 8, axis=0)
    rel = jnp.concatenate([rel, jnp.zeros((R, 512 - W), F32)], axis=1).T[:W]
    part = lax.broadcasted_iota(jnp.int32, (W, R), 1) // 16
    hi = rel.astype(BF16).astype(F32)
    mid = (rel - hi).astype(BF16).astype(F32)
    low = rel - hi - mid
    rel_ref[...] = jnp.where(part == 0, hi, jnp.where(part == 1, mid, jnp.where(part == 2, low, 0.0))).astype(BF16)


def pack_call(pos, count, neg, table, lhs, rhs, relidx, relation):
    smem = pl.BlockSpec(memory_space=pltpu.SMEM)
    vmem = pl.BlockSpec(memory_space=pltpu.VMEM)
    return pl.pallas_call(
        pack_kernel,
        out_shape=[
            jax.ShapeDtypeStruct((W + PACK, R), F32),
            jax.ShapeDtypeStruct((W, R), BF16),
            jax.ShapeDtypeStruct((2 * 16,), jnp.int32),
        ],
        in_specs=[smem] * 3 + [vmem] * 5,
        out_specs=[vmem, vmem, smem],
        name="pack",
    )(pos, count, neg, table, lhs, rhs, relidx, relation)


def last_kernel(pk_ref, lhs_ref, acc_ref, ent_ref, state_ref):
    tails = pk_ref[:, 3 * SLOT :, :].reshape(N_SHARD * 8, R)
    names = tails.T
    iota = lax.broadcasted_iota(jnp.int32, (R, N_SHARD * 8), 0).astype(F32)
    lane = lax.broadcasted_iota(jnp.int32, (N_SHARD * 8, R), 1)
    total = jnp.zeros((R, 512), F32)
    for k in range(SLOT // 8):
        oh = onehot(iota == names[96 + k : 97 + k, :])
        tail = tails if k == 0 else pltpu.roll(tails, R - 16 * k, 1)
        blocks = [pk_ref[:, b * SLOT + 8 * k : b * SLOT + 8 * k + 8, :].reshape(N_SHARD * 8, R) for b in range(3)]
        hi, lo = split(jnp.concatenate(blocks + [jnp.where(lane < 16, tail, 0.0)], axis=1))
        total += dot(oh, hi) + dot(oh, lo)
    g = total.T[:W] + lhs_ref[:W, :]
    state_ref[...] = acc_ref[...] + jnp.sum(g * g, axis=0, keepdims=True) * (1.0 / W)
    ent_ref[...] = g


def step_pairs(first, second):
    pairs = []
    for s in range(N_SHARD):
        x, y, c = s // 8, (s // 2) % 4, s % 2
        dx, dy = (first, second) if c == 0 else (second, first)
        pairs.append((s, (((x + dx) % 4) * 4 + (y + dy) % 4) * 2 + c))
    return pairs


def move(value, first=0, second=0):
    return lax.ppermute(value, "shard", step_pairs(first, second))


def swap_core(value):
    return lax.ppermute(value, "shard", [(s, s ^ 1) for s in range(N_SHARD)])


def swap_dom(value, mask):
    return lax.ppermute(value, "dom", [(d, d ^ mask) for d in range(N_DOM)])


def pair_move(value, mask):
    return lax.switch(mask - 1, [functools.partial(swap_dom, mask=m) for m in range(1, N_DOM)], value)


def after(value, first):
    return value + jnp.minimum(jnp.abs(first), 0.0)


def gather_tables(t, pack, mask):
    payload, rel, slots = pack(t)
    x1 = jnp.stack([payload[:W], move(t, first=-1), move(t, first=2), move(t, first=1)])
    z = pair_move(payload, mask)
    o1, o3 = move(x1, second=-1), move(x1, second=1)
    f2, g2 = move(after(o3[:2], z[:W]), second=1), move(after(o1[2:], z[:W]), second=-1)
    own = [x1, o1, o3, f2, g2]
    return slots, z, rel, own + [swap_core(v) for v in own]


def sum_shard(value, masks):
    others = [lax.ppermute(value, "shard", [(s, s ^ mask) for s in range(N_SHARD)]) for mask in masks]
    value = value + others[0]
    return value + (others[1] + others[2]) if len(masks) == 3 else value


def move_back(lhs, rel, mask):
    other = swap_dom(jnp.concatenate([lhs, rel]), mask)
    rel = rel + other[W:]
    for step in {1: (2, 6), 2: (1, 6), 3: (1, 6)}.get(mask, (1, 2)):
        rel = rel + swap_dom(rel, step)
    return other, rel


def local(embedding, accumulator, relation, plan, lhs_index, rhs_index, rel_index, slot_count, neg_span):
    shard = lax.axis_index("shard")
    pos = jnp.stack([shard // 8, (shard // 2) % 4, shard % 2]).astype(jnp.int32)
    mask = plan[0]
    table = embedding.T
    rows = (E // R, R)

    def pack(first):
        indices = [v.reshape(rows) for v in (lhs_index, rhs_index, rel_index)]
        return pack_call(pos, slot_count, neg_span, first, *indices, relation)

    slots, z, rel, pieces = gather_tables(table, pack, mask)
    packed, lhs_grad, rel_grad = main_call(slots, z, rel, pieces)
    returned = lax.all_to_all(packed, "shard", 0, 0, tiled=True)
    back = [functools.partial(move_back, mask=m) for m in range(1, N_DOM)]
    lhs_grad, rel_grad = lax.switch(mask - 1, back, lhs_grad, rel_grad)
    rel_grad = sum_shard(sum_shard(rel_grad, (1,)), (2, 4, 6))
    rel_grad = after(rel_grad, returned[0, :64])
    entity_grad, state = call(last_kernel, [(W, R), (1, R)], "last")(returned, lhs_grad, accumulator.reshape(1, R))
    rel_grad = after(sum_shard(rel_grad, (8, 16, 24)), entity_grad[:64])
    relation_grad = jnp.concatenate([rel_grad[:16], rel_grad[16:32], rel_grad[32:48], rel_grad[48:, : W - 3 * R]], axis=1)
    return entity_grad.T, state.reshape(R), relation_grad


def solution(mesh):
    both = P(("dom", "shard"))
    rows = P(("dom", "shard"), None)
    in_specs = (rows, both, P(), P(), both, both, both, rows, both)
    return jax.shard_map(local, mesh=mesh, in_specs=in_specs, out_specs=(rows, both, P()), check_vma=False)
```

```python
import functools

import jax
import jax.numpy as jnp
from jax import lax
from jax.experimental import pallas as pl
from jax.experimental.pallas import tpu as pltpu
from jax.sharding import PartitionSpec as P

W = 400
R = 128
E = 1536
CH = 512
SLOT = 48
SPANS = 3
N_DOM = 8
N_SHARD = 32
TILE = 256
TILES = E // TILE
SPREAD = 6
FIRST = [TILE * j // SLOT for j in range(TILES)]
PACK = 56
F32 = jnp.float32
BF16 = jnp.bfloat16
NT = (((1,), (1,)), ((), ()))
NN = (((1,), (0,)), ((), ()))


def dot(a, b, dims=NN):
    return lax.dot_general(a, b, dims, preferred_element_type=F32)


def split(x):
    hi = x.astype(BF16)
    return hi, (x - hi.astype(F32)).astype(BF16)


def onehot(mask):
    return jnp.where(mask, 1.0, 0.0).astype(BF16)


def row_at(z_ref, first, index):
    return z_ref[pl.ds(first + index, 1), :]


def rows_of(z_ref, first, j, count=2):
    return jnp.concatenate([row_at(z_ref, first, count * j + i) for i in range(count)], axis=1)


def columns(row):
    return jnp.broadcast_to(row, (R, R)).T


def main_kernel(slot_ref, z_ref, rel_ref, *refs):
    pieces = refs[:10]
    pk_ref, lg_ref, rg_ref = refs[10:13]
    hi_s, lo_s, lhs_s, rel_s, rhs_s, gl_s, gr_s, lhsb_s, rhsb_s, lhsr_s, rhsr_s, bias_s, rows_s, idx_s, rel_acc = refs[13:]

    for side in range(2):
        for piece, places in zip(pieces[5 * side : 5 * side + 5], PLACES):

            def one_table(i, _, piece=piece, first=16 * side + places[0]):
                lanes = pl.ds(pl.multiple_of(slot_ref[first + i] * R, R), R)
                hi, lo = split(piece[i])
                hi_s[:, lanes] = hi
                lo_s[:, lanes] = lo
                return 0

            lax.fori_loop(0, len(places), one_table, 0, unroll=2)

    lt_hi, lt_lo = split(z_ref[:W, :])
    sub_iota = lax.broadcasted_iota(jnp.int32, (SPREAD * R, TILE), 0).astype(F32)
    pad = jnp.zeros((512 - W, TILE), F32)
    rel_iota = lax.broadcasted_iota(jnp.int32, (R, TILE), 0)
    rel_iota = jnp.where(rel_iota < 48, rel_iota % 16, -1).astype(F32)
    rel3 = rel_ref[...]

    def one_tile(j, _):
        c = j // 2
        at = pl.multiple_of((j % 2) * TILE, TILE)
        lanes = pl.ds(at, TILE)
        base = (j * TILE // SLOT) * R
        start = base.astype(F32)
        cols = pl.ds(pl.multiple_of(base, R), SPREAD * R)
        oh = onehot(sub_iota == rows_of(z_ref, W + 12, j) - start)
        hi = hi_s[:, cols]
        rhs = dot(hi, oh) + dot(lo_s[:, cols], oh)
        rhs_s[c, :, lanes] = rhs
        rhsb_s[c, :, lanes] = rhs.astype(BF16)
        named = [columns(row_at(z_ref, W + 12, 2 * j + i)) for i in range(2)]
        rhsr_s[c, lanes, :] = jnp.concatenate([rhs, pad], axis=0).T[:, :W].astype(BF16)
        idx_s[pl.ds(pl.multiple_of(j * TILE, TILE), TILE), :] = jnp.concatenate(named, axis=0)
        oh = onehot(sub_iota[:R] == rows_of(z_ref, W, j))
        lhs = dot(lt_hi, oh) + dot(lt_lo, oh)
        lhs_s[c, :, lanes] = lhs
        lhsb_s[c, :, lanes] = lhs.astype(BF16)
        lhsr_s[c, lanes, :] = jnp.concatenate([lhs, pad], axis=0).T[:, :W].astype(BF16)
        oh = onehot(rel_iota == rows_of(z_ref, W + 24, j))
        rel_s[c, :, lanes] = dot(rel3, oh)
        live = jnp.concatenate([columns(row_at(z_ref, W + 36, 2 * j + i)) for i in range(2)], axis=0)
        bias_s[c, lanes, :] = jnp.where(live > 0.5, 0.0, -jnp.inf)
        return 0

    lax.fori_loop(0, TILES, one_tile, 0, unroll=6)

    gl_s[...] = jnp.zeros_like(gl_s)
    gr_s[...] = jnp.zeros_like(gr_s)
    rel_acc[...] = jnp.zeros_like(rel_acc)
    neg_row = z_ref[W + 48 : W + 49, :]
    lane_row = lax.broadcasted_iota(jnp.int32, (1, R), 1)
    rel_rows = lax.broadcasted_iota(jnp.int32, (16, CH), 0).astype(F32)

    def one_block(c, _):
        n = jnp.sum(jnp.where(lane_row == c, neg_row, 0.0)).astype(jnp.int32)
        lhs, rel, rhs = lhs_s[c], rel_s[c], rhs_s[c]
        left, right = lhs * rel, rhs * rel
        positive = jnp.sum(left * rhs, axis=0, keepdims=True)
        leftb, rightb = left.astype(BF16), right.astype(BF16)
        live = rows_of(z_ref, W + 36, c, 4)
        bias = jnp.concatenate([bias_s[n]] * 4, axis=1)

        def soft(neg_rows, edges):
            scores = dot(neg_rows, edges) + bias
            top = jnp.maximum(positive, jnp.max(scores, axis=0, keepdims=True))
            own = jnp.exp(positive - top)
            others = jnp.exp(scores - top)
            inv = 1.0 / (own + jnp.sum(others, axis=0, keepdims=True))
            return (others * (live * inv)).astype(BF16), own * inv

        tail_w, q_tail = soft(rhsr_s[n], leftb)
        head_w, q_head = soft(lhsr_s[n], rightb)
        weight = live * (q_tail + q_head - 2.0)
        grad_left = weight * rhs + dot(rhsb_s[n], tail_w)
        grad_right = dot(lhsb_s[n], head_w)
        gl_s[c] += grad_left * rel
        gr_s[c] += weight * left + grad_right * rel
        gr_s[n] += dot(leftb, tail_w, NT)
        gl_s[n] += dot(rightb, head_w, NT)
        ghi, glo = split(grad_left * lhs + grad_right * rhs)
        oh = onehot(rel_rows == rows_of(z_ref, W + 24, c, 4))
        rel_acc[...] += dot(oh, ghi, NT) + dot(oh, glo, NT)
        return 0

    lax.fori_loop(0, SPANS, one_block, 0, unroll=1)
    rel_grad = rel_acc[...]
    tail = jnp.concatenate([rel_grad[:, 384:], jnp.zeros((16, R - 16), F32)], axis=1)
    rg_ref[...] = jnp.concatenate([rel_grad[:, :R], rel_grad[:, R : 2 * R], rel_grad[:, 2 * R : 3 * R], tail], axis=0)

    lg_ref[...] = jnp.zeros_like(lg_ref)

    def one_sum(j, _):
        c = j // 2
        lanes = pl.ds(pl.multiple_of((j % 2) * TILE, TILE), TILE)
        oh = onehot(sub_iota[:R] == rows_of(z_ref, W, j))
        hi, lo = split(gl_s[c, :, lanes])
        lg_ref[...] += dot(hi, oh, NT) + dot(lo, oh, NT)
        rows = pl.ds(pl.multiple_of(j * TILE, TILE), TILE)
        rows_s[rows, :] = jnp.concatenate([gr_s[c, :, lanes], pad], axis=0).T
        return 0

    lax.fori_loop(0, TILES, one_sum, 0, unroll=3)
    lane = lax.broadcasted_iota(jnp.int32, (8, R), 1)

    def one_slot(o, _):
        first = pl.multiple_of(o * SLOT, SLOT)
        for k in range(3):
            pk_ref[o, k * SLOT : (k + 1) * SLOT, :] = rows_s[pl.ds(first, SLOT), k * R : (k + 1) * R]
        tail = jnp.zeros((8, R), F32)
        base = (o * R).astype(F32)
        for k in range(SLOT // 8):
            at = pl.ds(pl.multiple_of(first + 8 * k, 8), 8)
            piece = rows_s[at, 3 * R :]
            tail += piece if k == 0 else pltpu.roll(piece, 16 * k, 1)
            tail = jnp.where(lane == 96 + k, idx_s[at, :] - base, tail)
        pk_ref[o, 3 * SLOT :, :] = tail
        return 0

    lax.fori_loop(0, N_SHARD, one_slot, 0, unroll=16)


PLACES = [(0, 1, 2, 3), (4, 5, 6, 7), (12, 13, 14, 15), (8, 9), (10, 11)]
BLOCK = 3 * SLOT + 8


def main_call(slots, z, rel, pieces):
    smem = pl.BlockSpec(memory_space=pltpu.SMEM)
    vmem = pl.BlockSpec(memory_space=pltpu.VMEM)
    big = pltpu.VMEM((SPANS, W, CH), F32)
    half = pltpu.VMEM((SPANS, W, CH), BF16)
    rows = pltpu.VMEM((SPANS, CH, W), BF16)
    return pl.pallas_call(
        main_kernel,
        out_shape=[jax.ShapeDtypeStruct((N_SHARD, BLOCK, R), F32), jax.ShapeDtypeStruct((W, R), F32), jax.ShapeDtypeStruct((64, R), F32)],
        in_specs=[smem] + [vmem] * 12,
        out_specs=[vmem] * 3,
        scratch_shapes=[
            pltpu.VMEM((W, N_SHARD * R), BF16),
            pltpu.VMEM((W, N_SHARD * R), BF16),
            big, big, big, big, big, half, half, rows, rows,
            pltpu.VMEM((SPANS, CH, R), F32),
            pltpu.VMEM((E, 512), F32),
            pltpu.VMEM((E, R), F32),
            pltpu.VMEM((16, W), F32),
        ],
        compiler_params=pltpu.CompilerParams(vmem_limit_bytes=46 * 1024 * 1024),
        cost_estimate=pl.CostEstimate(flops=12_000_000_000, bytes_accessed=14_000_000, transcendentals=1_600_000),
        name="edges",
    )(slots, z, rel, *pieces)


def call(kernel, shapes, name):
    return pl.pallas_call(kernel, out_shape=[jax.ShapeDtypeStruct(v, F32) for v in shapes], name=name)


def pack_kernel(pos_ref, count_ref, neg_ref, table_ref, lhs_ref, rhs_ref, relidx_ref, relation_ref, z_ref, rel_ref, slot_ref):
    x, y, c = pos_ref[0], pos_ref[1], pos_ref[2]
    for side in range(2):
        core = c if side == 0 else 1 - c
        for place in range(16):
            jq, jp = divmod(place, 4)
            dx = jnp.where(core == 0, jp, jq)
            dy = jnp.where(core == 0, jq, jp)
            slot_ref[16 * side + place] = (((x + dx) & 3) * 4 + ((y + dy) & 3)) * 2 + core
    z_ref[:W, :] = table_ref[...]
    shape = (E // R, R)
    edge = lax.broadcasted_iota(jnp.int32, shape, 0) * R + lax.broadcasted_iota(jnp.int32, shape, 1)
    owner = jnp.zeros(shape, jnp.int32)
    live = jnp.zeros(shape, jnp.int32)
    for o in range(N_SHARD):
        inside = jnp.where(edge >= o * SLOT, 1, 0)
        owner = owner + inside
        live = live + inside * jnp.where(edge < o * SLOT + count_ref[0, o], 1, 0) * jnp.where(edge < (o + 1) * SLOT, 1, 0)
    z_ref[W : W + 12, :] = lhs_ref[...].astype(F32)
    z_ref[W + 12 : W + 24, :] = ((owner - 1) * R + rhs_ref[...]).astype(F32)
    z_ref[W + 24 : W + 36, :] = relidx_ref[...].astype(F32)
    z_ref[W + 36 : W + 48, :] = live.astype(F32)
    lane = lax.broadcasted_iota(jnp.int32, (PACK - 48, R), 1)
    neg = jnp.zeros((PACK - 48, R), jnp.int32)
    for c in range(SPANS):
        neg = jnp.where(lane == c, neg_ref[c], neg)
    z_ref[W + 48 :, :] = neg.astype(F32)
    rel = jnp.concatenate([relation_ref[...]] * 8, axis=0)
    rel = jnp.concatenate([rel, jnp.zeros((R, 512 - W), F32)], axis=1).T[:W]
    part = lax.broadcasted_iota(jnp.int32, (W, R), 1) // 16
    hi = rel.astype(BF16).astype(F32)
    mid = (rel - hi).astype(BF16).astype(F32)
    low = rel - hi - mid
    rel_ref[...] = jnp.where(part == 0, hi, jnp.where(part == 1, mid, jnp.where(part == 2, low, 0.0))).astype(BF16)


def pack_call(pos, count, neg, table, lhs, rhs, relidx, relation):
    smem = pl.BlockSpec(memory_space=pltpu.SMEM)
    vmem = pl.BlockSpec(memory_space=pltpu.VMEM)
    return pl.pallas_call(
        pack_kernel,
        out_shape=[
            jax.ShapeDtypeStruct((W + PACK, R), F32),
            jax.ShapeDtypeStruct((W, R), BF16),
            jax.ShapeDtypeStruct((2 * 16,), jnp.int32),
        ],
        in_specs=[smem] * 3 + [vmem] * 5,
        out_specs=[vmem, vmem, smem],
        name="pack",
    )(pos, count, neg, table, lhs, rhs, relidx, relation)


def last_kernel(pk_ref, lhs_ref, acc_ref, ent_ref, state_ref):
    tails = pk_ref[:, 3 * SLOT :, :].reshape(N_SHARD * 8, R)
    names = tails.T
    iota = lax.broadcasted_iota(jnp.int32, (R, N_SHARD * 8), 0).astype(F32)
    lane = lax.broadcasted_iota(jnp.int32, (N_SHARD * 8, R), 1)
    total = jnp.zeros((R, 512), F32)
    for k in range(SLOT // 8):
        oh = onehot(iota == names[96 + k : 97 + k, :])
        tail = tails if k == 0 else pltpu.roll(tails, R - 16 * k, 1)
        blocks = [pk_ref[:, b * SLOT + 8 * k : b * SLOT + 8 * k + 8, :].reshape(N_SHARD * 8, R) for b in range(3)]
        hi, lo = split(jnp.concatenate(blocks + [jnp.where(lane < 16, tail, 0.0)], axis=1))
        total += dot(oh, hi) + dot(oh, lo)
    g = total.T[:W] + lhs_ref[:W, :]
    state_ref[...] = acc_ref[...] + jnp.sum(g * g, axis=0, keepdims=True) * (1.0 / W)
    ent_ref[...] = g


def step_pairs(first, second):
    pairs = []
    for s in range(N_SHARD):
        x, y, c = s // 8, (s // 2) % 4, s % 2
        dx, dy = (first, second) if c == 0 else (second, first)
        pairs.append((s, (((x + dx) % 4) * 4 + (y + dy) % 4) * 2 + c))
    return pairs


def move(value, first=0, second=0):
    return lax.ppermute(value, "shard", step_pairs(first, second))


def swap_core(value):
    return lax.ppermute(value, "shard", [(s, s ^ 1) for s in range(N_SHARD)])


def swap_dom(value, mask):
    return lax.ppermute(value, "dom", [(d, d ^ mask) for d in range(N_DOM)])


def pair_move(value, mask):
    return lax.switch(mask - 1, [functools.partial(swap_dom, mask=m) for m in range(1, N_DOM)], value)


def after(value, first):
    return value + jnp.minimum(jnp.abs(first), 0.0)


def gather_tables(t, pack, mask):
    payload, rel, slots = pack(t)
    x1 = jnp.stack([payload[:W], move(t, first=-1), move(t, first=2), move(t, first=1)])
    z = pair_move(payload, mask)
    o1, o3 = move(x1, second=-1), move(x1, second=1)
    f2, g2 = move(after(o3[:2], z[:W]), second=1), move(after(o1[2:], z[:W]), second=-1)
    own = [x1, o1, o3, f2, g2]
    return slots, z, rel, own + [swap_core(v) for v in own]


def sum_shard(value, masks):
    others = [lax.ppermute(value, "shard", [(s, s ^ mask) for s in range(N_SHARD)]) for mask in masks]
    value = value + others[0]
    return value + (others[1] + others[2]) if len(masks) == 3 else value


def move_back(lhs, rel, mask):
    other = swap_dom(jnp.concatenate([lhs, rel]), mask)
    rel = rel + other[W:]
    for step in {1: (2, 6), 2: (1, 6), 3: (1, 6)}.get(mask, (1, 2)):
        rel = rel + swap_dom(rel, step)
    return other, rel


def local(embedding, accumulator, relation, plan, lhs_index, rhs_index, rel_index, slot_count, neg_span):
    shard = lax.axis_index("shard")
    pos = jnp.stack([shard // 8, (shard // 2) % 4, shard % 2]).astype(jnp.int32)
    mask = plan[0]
    table = embedding.T
    rows = (E // R, R)

    def pack(first):
        indices = [v.reshape(rows) for v in (lhs_index, rhs_index, rel_index)]
        return pack_call(pos, slot_count, neg_span, first, *indices, relation)

    slots, z, rel, pieces = gather_tables(table, pack, mask)
    packed, lhs_grad, rel_grad = main_call(slots, z, rel, pieces)
    returned = lax.all_to_all(packed, "shard", 0, 0, tiled=True)
    back = [functools.partial(move_back, mask=m) for m in range(1, N_DOM)]
    lhs_grad, rel_grad = lax.switch(mask - 1, back, lhs_grad, rel_grad)
    rel_grad = sum_shard(sum_shard(rel_grad, (1,)), (2, 4, 6))
    rel_grad = after(rel_grad, returned[0, :64])
    entity_grad, state = call(last_kernel, [(W, R), (1, R)], "last")(returned, lhs_grad, accumulator.reshape(1, R))
    rel_grad = after(sum_shard(rel_grad, (8, 16, 24)), entity_grad[:64])
    relation_grad = jnp.concatenate([rel_grad[:16], rel_grad[16:32], rel_grad[32:48], rel_grad[48:, : W - 3 * R]], axis=1)
    return entity_grad.T, state.reshape(R), relation_grad


def solution(mesh):
    both = P(("dom", "shard"))
    rows = P(("dom", "shard"), None)
    in_specs = (rows, both, P(), P(), both, both, both, rows, both)
    return jax.shard_map(local, mesh=mesh, in_specs=in_specs, out_specs=(rows, both, P()), check_vma=False)
```
